768 devices in a mesh: row: 24 (over y, z_hi), col: 32 (over x, z_lo, core).
Axes of the slice: x: 4, y: 8, z: 12 (z_hi: 3, z_lo: 4; z = z_hi * 4 + z_lo), core: 2. Of those that a mesh axis runs over, the one named last changes fastest.
Arguments:
- row_points: bfloat16 [24576, 64], P(('row', 'col')), may hold values from -0.75 to 0.75
- row_solves: bfloat16 [24576, 32], P(('row', 'col')), may hold values from -96 to 96
- col_points: bfloat16 [245760, 64], P(('col', 'row')), may hold values from -0.75 to 0.75
- col_probes: bfloat16 [245760, 32], P(('col', 'row')), may hold values from -6 to 6
Outputs:
- row_grad: float32 [24576, 64], P(('row', 'col'))
- col_grad: float32 [245760, 64], P(('col', 'row'))
The draws below stay inside these ranges and needn't reach their ends.
All inputs are finite; a program needn't handle non-finite values.
Results may differ from the reference program's by a relative error of at most 0.007.
Values may be sent and summed in bfloat16 or wider, within the bound.
No kernel may reach another device: no remote copies, remote signals or barrier semaphores. Data moves between devices by JAX's collectives and lax.ppermute only.
A program may use at most 32 MiB of HBM per device.

```python
import jax
import jax.numpy as jnp
from jax import lax

F = 64
P_SIZE = 32
COL_PIECE = 320
ROWS = 24576
COLS = 245760


def block_levels(stream_key, shape, split, low, high):
    loudness, own = 1.0, jax.random.fold_in(stream_key, 6)
    for dim, parts in split:
        steps = jnp.exp(jax.random.uniform(jax.random.fold_in(own, dim), (parts,), jnp.float32, low / len(split), high / len(split)))
        loudness = loudness * jnp.repeat(steps, shape[dim] // parts).reshape([-1 if axis == dim else 1 for axis in range(len(shape))])
    return loudness


def scatter_about(rng, dims, width, most, split=(), kind=jnp.bfloat16):
    drawn = width * jax.random.normal(rng, dims, jnp.float32)
    if split:
        drawn = drawn * block_levels(rng, dims, split, -0.22, 0.18)
    return jnp.clip(drawn, -most, most).astype(kind)


def setup_inputs(seed: int = 0) -> dict:
    arg_keys = jax.random.split(jax.random.key(seed), 5)
    return {
        "row_points": scatter_about(arg_keys[0], (ROWS, F), 0.3, 0.75, ((0, 768),)),
        "row_solves": scatter_about(arg_keys[1], (ROWS, P_SIZE), 16.0, 96.0, ((0, 768),)),
        "col_points": scatter_about(arg_keys[2], (COLS, F), 0.3, 0.75, ((0, 768),)),
        "col_probes": scatter_about(arg_keys[3], (COLS, P_SIZE), 1.0, 6.0, ((0, 768),)),
    }


def tile_weight(row_feat, row_norm, row_solve, col_feat, col_probe):
    gram = jnp.dot(row_feat, col_feat.T, preferred_element_type=jnp.float32)
    col_wide = col_feat.astype(jnp.float32)
    col_norm = jnp.sum(col_wide * col_wide, axis=1)
    kernel = jnp.exp(-0.5 * (row_norm[:, None] + col_norm[None, :] - 2.0 * gram))
    mixing = jnp.dot(row_solve, col_probe.T, preferred_element_type=jnp.float32) * (1.0 / P_SIZE)
    return (kernel * mixing).astype(jnp.bfloat16), col_wide


def reference(row_points, row_solves, col_points, col_probes):
    row_wide = row_points.astype(jnp.float32)
    row_norm = jnp.sum(row_wide * row_wide, axis=1)
    blocks = COLS // COL_PIECE
    feat_blocks = col_points.reshape(blocks, COL_PIECE, F)
    probe_blocks = col_probes.reshape(blocks, COL_PIECE, P_SIZE)

    def advance(carry, block):
        col_feat, col_probe = block
        weight, col_wide = tile_weight(row_points, row_norm, row_solves, col_feat, col_probe)
        wide = weight.astype(jnp.float32)
        row_part = jnp.dot(weight, col_feat, preferred_element_type=jnp.float32)
        col_part = jnp.dot(weight.T, row_points, preferred_element_type=jnp.float32)
        col_term = col_part - jnp.sum(wide, axis=0)[:, None] * col_wide
        return (carry[0] + row_part, carry[1] + jnp.sum(wide, axis=1)), col_term

    start = (jnp.zeros((ROWS, F), jnp.float32), jnp.zeros((ROWS,), jnp.float32))
    (row_acc, row_total), col_terms = lax.scan(advance, start, (feat_blocks, probe_blocks))
    row_grad = row_acc - row_total[:, None] * row_wide
    col_grad = col_terms.reshape(COLS, F)
    return row_grad, col_grad
```

```python
import jax
import jax.numpy as jnp
from jax import lax
from jax.experimental import pallas as pl
from jax.experimental.pallas import tpu as pltpu
from jax.sharding import Mesh, PartitionSpec as P

f32, bf16 = jnp.float32, jnp.bfloat16

NAMES = ("y", "zh", "x", "zl", "core")
SIZES = (8, 3, 4, 4, 2)
Z = ("zh", "zl")
NY, NZ, NC = 8, 12, 8
PR, PC, F, Q = 32, 320, 64, 32
R, C = PR * NY * NZ, PC * NC
NORM, ONES = F + Q, F + Q + 3
BI, BJ = 256, 512

VM = pl.BlockSpec(memory_space=pltpu.VMEM)


def thirds(v):
    a = v.astype(bf16)
    v = v - a.astype(f32)
    b = v.astype(bf16)
    return a, b, (v - b.astype(f32)).astype(bf16)


def pack_kernel(rp_ref, rs_ref, cp_ref, cq_ref, row_ref, col_ref):
    r = rp_ref[...].astype(f32)
    n = -0.5 * jnp.sum(r * r, axis=1, keepdims=True)
    ext = jnp.concatenate(
        [p.astype(f32) for p in thirds(n)] + [jnp.ones((PR, 3), f32), jnp.zeros((PR, 128 - ONES - 3), f32)], axis=1
    )
    rec = jnp.concatenate([r, rs_ref[...].astype(f32), ext], axis=1).astype(bf16)
    for k in range(NZ):
        row_ref[k] = rec
    c = jnp.concatenate([cp_ref[...].astype(f32), cq_ref[...].astype(f32) * (1.0 / Q)], axis=0)
    half = jnp.concatenate([c[:48, 256:], c[48:, 256:]], axis=1)
    piece = jnp.concatenate([c[:, :128], c[:, 128:256], half], axis=0).astype(bf16)
    for k in range(NC):
        col_ref[k] = piece


def main_kernel(r_ref, p_ref, row_ref, col_ref, acc_r, acc_c, rt, ct, ce, cm, cn, w_ref):
    for d in range(0, NC, 2):
        for e in (d, d + 1):
            ct[:96, (2 * e) * 128:(2 * e + 1) * 128] = p_ref[e, :96]
            ct[:96, (2 * e + 1) * 128:(2 * e + 2) * 128] = p_ref[e, 96:192]
        a, b = p_ref[d, 192:240], p_ref[d + 1, 192:240]
        at = (2 * NC + d // 2) * 128
        ct[:48, at:at + 128] = jnp.concatenate([a[:, :64], b[:, :64]], axis=1)
        ct[48:96, at:at + 128] = jnp.concatenate([a[:, 64:], b[:, 64:]], axis=1)
    wide = ct[:F, :].astype(f32)
    n = -0.5 * jnp.sum(wide * wide, axis=0, keepdims=True)
    ct[96:128, :] = jnp.concatenate(
        [jnp.ones((3, C), f32)] + [p.astype(f32) for p in thirds(n)] + [jnp.zeros((26, C), f32)], axis=0
    ).astype(bf16)
    ce[...] = ct[...]
    ce[F:F + Q, :] = jnp.zeros((Q, C), bf16)
    cm[...] = jnp.zeros_like(cm)
    cm[F:F + Q, :] = ct[F:F + Q, :]
    cn[...] = ce[...].T
    rt[...] = r_ref[...].T
    acc_c[...] = jnp.zeros_like(acc_c)

    def step(i, carry):
        at = pl.multiple_of(i * BI, BI)
        r = r_ref[pl.ds(at, BI), :]
        for j in range(0, C, BJ):
            e = jnp.dot(r, ce[:, j:j + BJ], preferred_element_type=f32)
            m = jnp.dot(r, cm[:, j:j + BJ], preferred_element_type=f32)
            w_ref[:, j:j + BJ] = (jnp.exp(e) * m).astype(bf16)
        for j in range(0, C, BJ):
            acc_c[:, j:j + BJ] += jnp.dot(rt[:, pl.ds(at, BI)], w_ref[:, j:j + BJ], preferred_element_type=f32)
        acc_r[pl.ds(at, BI), :] = jnp.dot(w_ref[...], cn[...], preferred_element_type=f32)
        return carry

    lax.fori_loop(0, R // BI, step, 0)

    a = acc_r[...]
    t = a[:, :F] - a[:, NORM:NORM + 1] * r_ref[:, :F].astype(f32)
    t = t.reshape(R // PR, 2, PR // 2, F)
    row_ref[...] = jnp.concatenate([t[:, 0], t[:, 1]], axis=-1).reshape(R // 2, 128).astype(bf16)
    u = acc_c[:F, :] - acc_c[ONES:ONES + 1, :] * ct[:F, :].astype(f32)
    for d in range(NC):
        col_ref[d, :64] = u[:, (2 * d) * 128:(2 * d + 1) * 128].astype(bf16)
        col_ref[d, 64:128] = u[:, (2 * d + 1) * 128:(2 * d + 2) * 128].astype(bf16)
        at = 2 * NC * 128 + d * 64
        h = u[:, at:at + 64]
        col_ref[d, 128:] = jnp.concatenate([h[:32], h[32:]], axis=1).astype(bf16)


def finish_kernel(row_ref, col_ref, rg_ref, cg_ref):
    s = jnp.sum(row_ref[...].astype(f32), axis=0)
    rg_ref[...] = jnp.concatenate([s[:, :F], s[:, F:]], axis=0)
    s = jnp.sum(col_ref[...].astype(f32), axis=0)
    half = jnp.concatenate([s[128:, :64], s[128:, 64:]], axis=0)
    cg_ref[...] = jnp.concatenate([s[:64], s[64:128], half], axis=1)


def body(row_points, row_solves, col_points, col_probes):
    shape = jax.ShapeDtypeStruct
    rows, cols = pl.pallas_call(
        pack_kernel,
        out_shape=(shape((NZ, PR, 128), bf16), shape((NC, 240, 128), bf16)),
        in_specs=[VM] * 4,
        out_specs=(VM, VM),
    )(row_points, row_solves, col_points.T, col_probes.T)
    rows = lax.all_to_all(rows, Z, 0, 0, tiled=True)
    cols = lax.all_to_all(cols, ("x", "core"), 0, 0, tiled=True)
    rows = jnp.broadcast_to(rows.reshape(1, NZ * PR, 128), (NY, NZ * PR, 128))
    rows = lax.all_to_all(rows, "y", 0, 0, tiled=True)
    row_part, col_part = pl.pallas_call(
        main_kernel,
        out_shape=(shape((R // 2, 128), bf16), shape((NC, 160, 128), bf16)),
        in_specs=[VM, VM],
        out_specs=(VM, VM),
        scratch_shapes=[
            pltpu.VMEM((R, 128), f32),
            pltpu.VMEM((128, C), f32),
            pltpu.VMEM((128, R), bf16),
            pltpu.VMEM((128, C), bf16),
            pltpu.VMEM((128, C), bf16),
            pltpu.VMEM((128, C), bf16),
            pltpu.VMEM((C, 128), bf16),
            pltpu.VMEM((BI, C), bf16),
        ],
        compiler_params=pltpu.CompilerParams(vmem_limit_bytes=40 * 2**20),
    )(rows.reshape(R, 128), cols)
    row_part = lax.all_to_all(row_part.reshape(NY, NZ * PR // 2, 128), "y", 0, 0, tiled=True)
    row_part = jnp.sum(row_part.astype(f32), axis=0).astype(bf16).reshape(NZ, PR // 2, 128)
    row_part = lax.all_to_all(row_part, Z, 0, 0, tiled=True)
    col_part = lax.all_to_all(col_part, ("x", "core"), 0, 0, tiled=True)
    row_grad, col_grad = pl.pallas_call(
        finish_kernel,
        out_shape=(shape((PR, F), f32), shape((F, PC), f32)),
        in_specs=[VM, VM],
        out_specs=(VM, VM),
    )(row_part, col_part)
    return row_grad, col_grad.T


def solution(mesh):
    rings = Mesh(mesh.devices.reshape(SIZES), NAMES)
    row = P(("y", "zh", "x", "zl", "core"), None)
    col = P(("x", "zl", "core", "y", "zh"), None)
    return jax.shard_map(
        body,
        mesh=rings,
        in_specs=(row, row, col, col),
        out_specs=(row, col),
        check_vma=False,
    )
```

```python
import jax
import jax.numpy as jnp
from jax import lax
from jax.experimental import pallas as pl
from jax.experimental.pallas import tpu as pltpu
from jax.sharding import Mesh, PartitionSpec as P

f32, bf16 = jnp.float32, jnp.bfloat16

NAMES = ("y", "zh", "x", "zl", "core")
SIZES = (8, 3, 4, 4, 2)
Z = ("zh", "zl")
NY, NZ, NC = 8, 12, 8
PR, PC, F, Q = 32, 320, 64, 32
R, C = PR * NY * NZ, PC * NC
NORM, ONES = F + Q, F + Q + 3
BI, BJ = 768, 512
PK = BI * 3 // 4

VM = pl.BlockSpec(memory_space=pltpu.VMEM)


def thirds(v):
    a = v.astype(bf16)
    v = v - a.astype(f32)
    b = v.astype(bf16)
    return a, b, (v - b.astype(f32)).astype(bf16)


def pack_kernel(rp_ref, rs_ref, cp_ref, cq_ref, row_ref, col_ref):
    r, s = rp_ref[...].astype(f32), rs_ref[...].astype(f32)
    rec = jnp.concatenate(
        [
            jnp.concatenate([r[:16], r[16:]], axis=1),
            jnp.concatenate([s[:8], s[8:16], s[16:24], s[24:]], axis=1),
        ],
        axis=0,
    ).astype(bf16)
    for k in range(NZ):
        row_ref[k] = rec
    c = jnp.concatenate([cp_ref[...].astype(f32), cq_ref[...].astype(f32) * (1.0 / Q)], axis=0)
    half = jnp.concatenate([c[:48, 256:], c[48:, 256:]], axis=1)
    col_ref[...] = jnp.concatenate([c[:, :128], c[:, 128:256], half], axis=0).astype(bf16)


def column_records(p_ref, ct, ce, cm, cn):
    for d in range(0, NC, 2):
        for e in (d, d + 1):
            ct[:96, (2 * e) * 128:(2 * e + 1) * 128] = p_ref[e, :96]
            ct[:96, (2 * e + 1) * 128:(2 * e + 2) * 128] = p_ref[e, 96:192]
        a, b = p_ref[d, 192:240], p_ref[d + 1, 192:240]
        at = (2 * NC + d // 2) * 128
        ct[:48, at:at + 128] = jnp.concatenate([a[:, :64], b[:, :64]], axis=1)
        ct[48:96, at:at + 128] = jnp.concatenate([a[:, 64:], b[:, 64:]], axis=1)
    wide = ct[:F, :].astype(f32)
    n = -0.5 * jnp.sum(wide * wide, axis=0, keepdims=True)
    ct[96:128, :] = jnp.concatenate(
        [jnp.ones((3, C), f32)] + [p.astype(f32) for p in thirds(n)] + [jnp.zeros((26, C), f32)], axis=0
    ).astype(bf16)
    ce[...] = ct[...]
    ce[F:F + Q, :] = jnp.zeros((Q, C), bf16)
    cm[...] = jnp.zeros_like(cm)
    cm[F:F + Q, :] = ct[F:F + Q, :]
    cn[...] = ce[...].T


def row_records(packed):
    n = packed.shape[0] // 24
    rec = packed.astype(f32).reshape(n, 24, 128)
    points, solves = rec[:, :16], rec[:, 16:]

    def roll(x, k):
        return pltpu.roll(x.reshape(-1, 128), k, 1).reshape(x.shape)

    r = jnp.stack([points, roll(points, 64)], axis=1).reshape(n * PR, 128)
    s = jnp.stack([roll(solves, 64), roll(solves, 32), solves, roll(solves, 96)], axis=1).reshape(n * PR, 128)
    lane = lax.broadcasted_iota(jnp.int32, (n * PR, 128), 1)
    r = jnp.where(lane < F, r, 0.0)
    a, b, c = [t.astype(f32) for t in thirds(-0.5 * jnp.sum(r * r, axis=1, keepdims=True))]
    ext = jnp.where(lane < ONES + 3, 1.0, 0.0)
    ext = jnp.where(lane == NORM, a, jnp.where(lane == NORM + 1, b, jnp.where(lane == NORM + 2, c, ext)))
    return r, jnp.where(lane < F, r, jnp.where(lane < NORM, s, ext)).astype(bf16)


def main_kernel(r_ref, p_ref, row_ref, col_ref, acc_c, ct, ce, cm, cn, w0, w1, rt0, rt1, rf0, rf1):
    column_records(p_ref, ct, ce, cm, cn)
    acc_c[...] = jnp.zeros_like(acc_c)
    bufs = ((w0, rt0, rf0), (w1, rt1, rf1))
    n = R // BI

    def front(i, buf):
        r, rb = row_records(r_ref[pl.ds(pl.multiple_of(i * PK, PK), PK), :])
        buf[1][...] = rb.T
        buf[2][...] = r
        return rb

    def weights(rb, j, buf):
        e = jnp.dot(rb, ce[:, j:j + BJ], preferred_element_type=f32)
        m = jnp.dot(rb, cm[:, j:j + BJ], preferred_element_type=f32)
        buf[0][:, j:j + BJ] = (jnp.exp(e) * m).astype(bf16)

    def columns(j, buf):
        acc_c[:, j:j + BJ] += jnp.dot(buf[1][...], buf[0][:, j:j + BJ], preferred_element_type=f32)

    def rows(i, buf):
        a = jnp.dot(buf[0][...], cn[...], preferred_element_type=f32)
        t = a[:, :F] - a[:, NORM:NORM + 1] * buf[2][:, :F]
        t = t.reshape(BI // PR, 2, PR // 2, F)
        row_ref[pl.ds(pl.multiple_of(i * BI // 2, BI // 2), BI // 2), :] = (
            jnp.concatenate([t[:, 0], t[:, 1]], axis=-1).reshape(BI // 2, 128).astype(bf16)
        )

    def both(i, new, old):
        rb = front(i, new)
        for j in range(0, C, BJ):
            weights(rb, j, new)
            columns(j, old)
        rows(i - 1, old)

    rb = front(0, bufs[0])
    for j in range(0, C, BJ):
        weights(rb, j, bufs[0])

    def step(k, carry):
        both(2 * k + 1, bufs[1], bufs[0])
        both(2 * k + 2, bufs[0], bufs[1])
        return carry

    lax.fori_loop(0, (n - 2) // 2, step, 0)
    both(n - 1, bufs[1], bufs[0])
    for j in range(0, C, BJ):
        columns(j, bufs[1])
    rows(n - 1, bufs[1])

    u = acc_c[:F, :] - acc_c[ONES:ONES + 1, :] * ct[:F, :].astype(f32)
    for d in range(NC):
        col_ref[d, :64] = u[:, (2 * d) * 128:(2 * d + 1) * 128]
        col_ref[d, 64:128] = u[:, (2 * d + 1) * 128:(2 * d + 2) * 128]
        at = 2 * NC * 128 + d * 64
        h = u[:, at:at + 64]
        col_ref[d, 128:] = jnp.concatenate([h[:32], h[32:]], axis=1)


def finish_kernel(row_ref, col_ref, rg_ref, cg_ref):
    s = jnp.sum(row_ref[...].astype(f32), axis=0)
    rg_ref[...] = jnp.concatenate([s[:, :F], s[:, F:]], axis=0)
    s = col_ref[...]
    half = jnp.concatenate([s[128:, :64], s[128:, 64:]], axis=0)
    cg_ref[...] = jnp.concatenate([s[:64], s[64:128], half], axis=1)


def body(row_points, row_solves, col_points, col_probes):
    shape = jax.ShapeDtypeStruct
    rows, cols = pl.pallas_call(
        pack_kernel,
        out_shape=(shape((NZ, 24, 128), bf16), shape((240, 128), bf16)),
        in_specs=[VM] * 4,
        out_specs=(VM, VM),
    )(row_points, row_solves, col_points.T, col_probes.T)
    rows = lax.all_to_all(rows, Z, 0, 0, tiled=True)
    cols = lax.all_gather(cols, ("x", "core"), axis=0, tiled=False)
    rows = jnp.broadcast_to(rows.reshape(1, NZ * 24, 128), (NY, NZ * 24, 128))
    rows = lax.all_to_all(rows, "y", 0, 0, tiled=True)
    row_part, col_part = pl.pallas_call(
        main_kernel,
        out_shape=(shape((R // 2, 128), bf16), shape((NC, 160, 128), f32)),
        in_specs=[VM, VM],
        out_specs=(VM, VM),
        scratch_shapes=[
            pltpu.VMEM((128, C), f32),
            pltpu.VMEM((128, C), bf16),
            pltpu.VMEM((128, C), bf16),
            pltpu.VMEM((128, C), bf16),
            pltpu.VMEM((C, 128), bf16),
            pltpu.VMEM((BI, C), bf16),
            pltpu.VMEM((BI, C), bf16),
            pltpu.VMEM((128, BI), bf16),
            pltpu.VMEM((128, BI), bf16),
            pltpu.VMEM((BI, 128), f32),
            pltpu.VMEM((BI, 128), f32),
        ],
        compiler_params=pltpu.CompilerParams(vmem_limit_bytes=40 * 2**20),
    )(rows.reshape(R * 3 // 4, 128), cols)
    row_part = lax.all_to_all(row_part.reshape(NY, NZ * PR // 2, 128), "y", 0, 0, tiled=True)
    row_part = jnp.sum(row_part.astype(f32), axis=0).astype(bf16).reshape(NZ, PR // 2, 128)
    row_part = lax.all_to_all(row_part, Z, 0, 0, tiled=True)
    col_part = lax.psum_scatter(col_part.reshape(NC * 160, 128), ("x", "core"), scatter_dimension=0, tiled=True)
    row_grad, col_grad = pl.pallas_call(
        finish_kernel,
        out_shape=(shape((PR, F), f32), shape((F, PC), f32)),
        in_specs=[VM, VM],
        out_specs=(VM, VM),
    )(row_part, col_part)
    return row_grad, col_grad.T


def solution(mesh):
    rings = Mesh(mesh.devices.reshape(SIZES), NAMES)
    row = P(("y", "zh", "x", "zl", "core"), None)
    col = P(("x", "zl", "core", "y", "zh"), None)
    return jax.shard_map(
        body,
        mesh=rings,
        in_specs=(row, row, col, col),
        out_specs=(row, col),
        check_vma=False,
    )
```

```python
import jax
import jax.numpy as jnp
from jax import lax
from jax.experimental import pallas as pl
from jax.experimental.pallas import tpu as pltpu
from jax.sharding import Mesh, PartitionSpec as P

f32, bf16 = jnp.float32, jnp.bfloat16

NAMES = ("y", "zh", "x", "zl", "core")
SIZES = (8, 3, 4, 4, 2)
Z = ("zh", "zl")
NX, NY, NZ, NC = 4, 8, 12, 8
PR, PC, F, Q = 32, 320, 64, 32
R, C = PR * NY * NZ, PC * NC
NORM, ONES = F + Q, F + Q + 3
BI, BJ = 768, 512
PK = BI * 3 // 4

VM = pl.BlockSpec(memory_space=pltpu.VMEM)
SMALL = pltpu.CompilerParams(vmem_limit_bytes=8 * 2**20)


def thirds(v):
    a = v.astype(bf16)
    v = v - a.astype(f32)
    b = v.astype(bf16)
    return a, b, (v - b.astype(f32)).astype(bf16)


def pack_kernel(rp_ref, rs_ref, cp_ref, cq_ref, row_ref, col_ref):
    r, s = rp_ref[...].astype(f32), rs_ref[...].astype(f32)
    rec = jnp.concatenate(
        [
            jnp.concatenate([r[:16], r[16:]], axis=1),
            jnp.concatenate([s[:8], s[8:16], s[16:24], s[24:]], axis=1),
        ],
        axis=0,
    ).astype(bf16)
    for k in range(NZ):
        row_ref[k] = rec
    c = jnp.concatenate([cp_ref[...].astype(f32), cq_ref[...].astype(f32) * (1.0 / Q)], axis=0)
    half = jnp.concatenate([c[:48, 256:], c[48:, 256:]], axis=1)
    col_ref[...] = jnp.concatenate([c[:, :128], c[:, 128:256], half], axis=0).astype(bf16)


def column_records(p_ref, ct, ce, cm, cn):
    for d in range(0, NC, 2):
        for e in (d, d + 1):
            ct[:96, (2 * e) * 128:(2 * e + 1) * 128] = p_ref[e, :96]
            ct[:96, (2 * e + 1) * 128:(2 * e + 2) * 128] = p_ref[e, 96:192]
        a, b = p_ref[d, 192:240], p_ref[d + 1, 192:240]
        at = (2 * NC + d // 2) * 128
        ct[:48, at:at + 128] = jnp.concatenate([a[:, :64], b[:, :64]], axis=1)
        ct[48:96, at:at + 128] = jnp.concatenate([a[:, 64:], b[:, 64:]], axis=1)
    wide = ct[:F, :].astype(f32)
    n = -0.5 * jnp.sum(wide * wide, axis=0, keepdims=True)
    ct[96:128, :] = jnp.concatenate(
        [jnp.ones((3, C), f32)] + [p.astype(f32) for p in thirds(n)] + [jnp.zeros((26, C), f32)], axis=0
    ).astype(bf16)
    ce[...] = ct[...]
    ce[F:F + Q, :] = jnp.zeros((Q, C), bf16)
    cm[...] = jnp.zeros_like(cm)
    cm[F:F + Q, :] = ct[F:F + Q, :]
    cn[...] = ce[...].T


def row_records(packed):
    n = packed.shape[0] // 24
    rec = packed.astype(f32).reshape(n, 24, 128)
    points, solves = rec[:, :16], rec[:, 16:]

    def roll(x, k):
        return pltpu.roll(x.reshape(-1, 128), k, 1).reshape(x.shape)

    r = jnp.stack([points, roll(points, 64)], axis=1).reshape(n * PR, 128)
    s = jnp.stack([roll(solves, 64), roll(solves, 32), solves, roll(solves, 96)], axis=1).reshape(n * PR, 128)
    lane = lax.broadcasted_iota(jnp.int32, (n * PR, 128), 1)
    r = jnp.where(lane < F, r, 0.0)
    a, b, c = [t.astype(f32) for t in thirds(-0.5 * jnp.sum(r * r, axis=1, keepdims=True))]
    ext = jnp.where(lane < ONES + 3, 1.0, 0.0)
    ext = jnp.where(lane == NORM, a, jnp.where(lane == NORM + 1, b, jnp.where(lane == NORM + 2, c, ext)))
    return r, jnp.where(lane < F, r, jnp.where(lane < NORM, s, ext)).astype(bf16)


def main_kernel(r_ref, p_ref, row_ref, keep_ref, swap_ref, acc_c, ct, ce, cm, cn, w0, w1, rt0, rt1, rf0, rf1):
    column_records(p_ref, ct, ce, cm, cn)
    acc_c[...] = jnp.zeros_like(acc_c)
    bufs = ((w0, rt0, rf0), (w1, rt1, rf1))
    n = R // BI

    def front(i, buf):
        r, rb = row_records(r_ref[pl.ds(pl.multiple_of(i * PK, PK), PK), :])
        buf[1][...] = rb.T
        buf[2][...] = r
        return rb

    def weights(rb, j, buf):
        e = jnp.dot(rb, ce[:, j:j + BJ], preferred_element_type=f32)
        m = jnp.dot(rb, cm[:, j:j + BJ], preferred_element_type=f32)
        buf[0][:, j:j + BJ] = (jnp.exp(e) * m).astype(bf16)

    def columns(j, buf):
        acc_c[:, j:j + BJ] += jnp.dot(buf[1][...], buf[0][:, j:j + BJ], preferred_element_type=f32)

    def rows(i, buf):
        a = jnp.dot(buf[0][...], cn[...], preferred_element_type=f32)
        t = a[:, :F] - a[:, NORM:NORM + 1] * buf[2][:, :F]
        t = t.reshape(BI // PR, 2, PR // 2, F)
        row_ref[pl.ds(pl.multiple_of(i * BI // 2, BI // 2), BI // 2), :] = (
            jnp.concatenate([t[:, 0], t[:, 1]], axis=-1).reshape(BI // 2, 128).astype(bf16)
        )

    def both(i, new, old):
        rb = front(i, new)
        for j in range(0, C, BJ):
            weights(rb, j, new)
            columns(j, old)
        rows(i - 1, old)

    rb = front(0, bufs[0])
    for j in range(0, C, BJ):
        weights(rb, j, bufs[0])

    def step(k, carry):
        both(2 * k + 1, bufs[1], bufs[0])
        both(2 * k + 2, bufs[0], bufs[1])
        return carry

    lax.fori_loop(0, (n - 2) // 2, step, 0)
    both(n - 1, bufs[1], bufs[0])
    for j in range(0, C, BJ):
        columns(j, bufs[1])
    rows(n - 1, bufs[1])

    u = acc_c[:F, :] - acc_c[ONES:ONES + 1, :] * ct[:F, :].astype(f32)

    def piece(d):
        h = u[:, 2 * NC * 128 + d * 64:2 * NC * 128 + d * 64 + 64]
        return jnp.concatenate(
            [
                u[:, (2 * d) * 128:(2 * d + 1) * 128],
                u[:, (2 * d + 1) * 128:(2 * d + 2) * 128],
                jnp.concatenate([h[:32], h[32:]], axis=1),
            ],
            axis=0,
        )

    x, core = lax.axis_index("x"), lax.axis_index("core")
    for i in range(NX):
        k = lax.rem(i - x + NX, NX)
        a, b = piece(2 * i), piece(2 * i + 1)
        keep_ref[k] = jnp.where(core == 0, a, b)
        swap_ref[k] = jnp.where(core == 0, b, a).astype(bf16)


def add_kernel(keep_ref, swap_ref, own_ref, *out_refs):
    own_ref[...] = keep_ref[0] + swap_ref[0].astype(f32)
    for k in range(1, NX):
        out_refs[k - 1][...] = (keep_ref[k] + swap_ref[k].astype(f32)).astype(bf16)


def finish_rows(row_ref, out_ref):
    s = jnp.sum(row_ref[...].astype(f32), axis=0)
    out_ref[...] = jnp.concatenate([s[:, :F], s[:, F:]], axis=0)


def finish_cols(own_ref, *refs):
    s = own_ref[...]
    for ref in refs[:-1]:
        s = s + ref[...].astype(f32)
    half = jnp.concatenate([s[128:, :64], s[128:, 64:]], axis=0)
    refs[-1][...] = jnp.concatenate([s[:64], s[64:128], half], axis=1)


def body(row_points, row_solves, col_points, col_probes):
    shape = jax.ShapeDtypeStruct
    rows, cols = pl.pallas_call(
        pack_kernel,
        out_shape=(shape((NZ, 24, 128), bf16), shape((240, 128), bf16)),
        in_specs=[VM] * 4,
        out_specs=(VM, VM),
    )(row_points, row_solves, col_points.T, col_probes.T)
    rows = lax.all_to_all(rows, Z, 0, 0, tiled=True)
    cols = lax.all_gather(cols, ("x", "core"), axis=0, tiled=False)
    rows = jnp.broadcast_to(rows.reshape(1, NZ * 24, 128), (NY, NZ * 24, 128))
    rows = lax.all_to_all(rows, "y", 0, 0, tiled=True)
    row_part, keep, swap = pl.pallas_call(
        main_kernel,
        out_shape=(shape((R // 2, 128), bf16), shape((NX, 160, 128), f32), shape((NX, 160, 128), bf16)),
        in_specs=[VM, VM],
        out_specs=(VM, VM, VM),
        scratch_shapes=[
            pltpu.VMEM((128, C), f32),
            pltpu.VMEM((128, C), bf16),
            pltpu.VMEM((128, C), bf16),
            pltpu.VMEM((128, C), bf16),
            pltpu.VMEM((C, 128), bf16),
            pltpu.VMEM((BI, C), bf16),
            pltpu.VMEM((BI, C), bf16),
            pltpu.VMEM((128, BI), bf16),
            pltpu.VMEM((128, BI), bf16),
            pltpu.VMEM((BI, 128), f32),
            pltpu.VMEM((BI, 128), f32),
        ],
        compiler_params=pltpu.CompilerParams(vmem_limit_bytes=40 * 2**20),
    )(rows.reshape(R * 3 // 4, 128), cols)
    row_part = lax.all_to_all(row_part.reshape(NY, NZ * PR // 2, 128), "y", 0, 0, tiled=True)
    row_part = jnp.sum(row_part.astype(f32), axis=0).astype(bf16).reshape(NZ, PR // 2, 128)
    row_part = lax.all_to_all(row_part, Z, 0, 0, tiled=True)
    swap = lax.ppermute(swap, "core", [(0, 1), (1, 0)])
    parts = pl.pallas_call(
        add_kernel,
        out_shape=(shape((160, 128), f32),) + (shape((160, 128), bf16),) * (NX - 1),
        in_specs=[VM, VM],
        out_specs=(VM,) * NX,
        compiler_params=SMALL,
    )(keep, swap)
    parts = [parts[0]] + [lax.ppermute(parts[k], "x", [(i, (i + k) % NX) for i in range(NX)]) for k in range(1, NX)]
    col_grad = pl.pallas_call(
        finish_cols,
        out_shape=shape((F, PC), f32),
        in_specs=[VM] * NX,
        out_specs=VM,
        compiler_params=SMALL,
    )(*parts)
    row_grad = pl.pallas_call(
        finish_rows,
        out_shape=shape((PR, F), f32),
        in_specs=[VM],
        out_specs=VM,
        compiler_params=SMALL,
    )(row_part)
    return row_grad, col_grad.T


def solution(mesh):
    rings = Mesh(mesh.devices.reshape(SIZES), NAMES)
    row = P(("y", "zh", "x", "zl", "core"), None)
    col = P(("x", "zl", "core", "y", "zh"), None)
    return jax.shard_map(
        body,
        mesh=rings,
        in_specs=(row, row, col, col),
        out_specs=(row, col),
        check_vma=False,
    )
```

```python
import jax
import jax.numpy as jnp
from jax import lax
from jax.experimental import pallas as pl
from jax.experimental.pallas import tpu as pltpu
from jax.sharding import Mesh, PartitionSpec as P

f32, bf16 = jnp.float32, jnp.bfloat16

NAMES = ("y", "zh", "x", "zl", "core")
SIZES = (8, 3, 4, 4, 2)
Z = ("zh", "zl")
NX, NY, NZ, NC = 4, 8, 12, 2
PR, PC, F, Q = 32, 320, 64, 32
R, C = PR * NX * NZ * NC, PC * NY
NORM, ONES = F + Q, F + Q + 3
BI, BJ = R // NX, 512
PK = BI * 3 // 4

VM = pl.BlockSpec(memory_space=pltpu.VMEM)
SMALL = pltpu.CompilerParams(vmem_limit_bytes=8 * 2**20)


def thirds(v):
    a = v.astype(bf16)
    v = v - a.astype(f32)
    b = v.astype(bf16)
    return a, b, (v - b.astype(f32)).astype(bf16)


def pack_kernel(rp_ref, rs_ref, cp_ref, cq_ref, row_ref, col_ref):
    r, s = rp_ref[...].astype(f32), rs_ref[...].astype(f32)
    rec = jnp.concatenate(
        [
            jnp.concatenate([r[:16], r[16:]], axis=1),
            jnp.concatenate([s[:8], s[8:16], s[16:24], s[24:]], axis=1),
        ],
        axis=0,
    ).astype(bf16)
    for k in range(NZ):
        row_ref[k] = rec
    c = jnp.concatenate([cp_ref[...].astype(f32), cq_ref[...].astype(f32) * (1.0 / Q)], axis=0)
    half = jnp.concatenate([c[:48, 256:], c[48:, 256:]], axis=1)
    piece = jnp.concatenate([c[:, :128], c[:, 128:256], half], axis=0).astype(bf16)
    for k in range(NY):
        col_ref[k] = piece


def column_records(p_ref, ct, ce, cm, cn):
    for d in range(0, NY, 2):
        for e in (d, d + 1):
            ct[:96, (2 * e) * 128:(2 * e + 1) * 128] = p_ref[e, :96]
            ct[:96, (2 * e + 1) * 128:(2 * e + 2) * 128] = p_ref[e, 96:192]
        a, b = p_ref[d, 192:240], p_ref[d + 1, 192:240]
        at = (2 * NY + d // 2) * 128
        ct[:48, at:at + 128] = jnp.concatenate([a[:, :64], b[:, :64]], axis=1)
        ct[48:96, at:at + 128] = jnp.concatenate([a[:, 64:], b[:, 64:]], axis=1)
    wide = ct[:F, :].astype(f32)
    n = -0.5 * jnp.sum(wide * wide, axis=0, keepdims=True)
    ct[96:128, :] = jnp.concatenate(
        [jnp.ones((3, C), f32)] + [p.astype(f32) for p in thirds(n)] + [jnp.zeros((26, C), f32)], axis=0
    ).astype(bf16)
    ce[...] = ct[...]
    ce[F:F + Q, :] = jnp.zeros((Q, C), bf16)
    cm[...] = jnp.zeros_like(cm)
    cm[F:F + Q, :] = ct[F:F + Q, :]
    cn[...] = ce[...].T


def row_records(packed):
    n = packed.shape[0] // 24
    rec = packed.astype(f32).reshape(n, 24, 128)
    points, solves = rec[:, :16], rec[:, 16:]

    def roll(x, k):
        return pltpu.roll(x.reshape(-1, 128), k, 1).reshape(x.shape)

    r = jnp.stack([points, roll(points, 64)], axis=1).reshape(n * PR, 128)
    s = jnp.stack([roll(solves, 64), roll(solves, 32), solves, roll(solves, 96)], axis=1).reshape(n * PR, 128)
    lane = lax.broadcasted_iota(jnp.int32, (n * PR, 128), 1)
    r = jnp.where(lane < F, r, 0.0)
    a, b, c = [t.astype(f32) for t in thirds(-0.5 * jnp.sum(r * r, axis=1, keepdims=True))]
    ext = jnp.where(lane < ONES + 3, 1.0, 0.0)
    ext = jnp.where(lane == NORM, a, jnp.where(lane == NORM + 1, b, jnp.where(lane == NORM + 2, c, ext)))
    return r, jnp.where(lane < F, r, jnp.where(lane < NORM, s, ext)).astype(bf16)


def main_kernel(r_ref, p_ref, keep_ref, swap_ref, col_ref, acc_c, ct, ce, cm, cn, w0, w1, rt0, rt1, rf0, rf1):
    column_records(p_ref, ct, ce, cm, cn)
    acc_c[...] = jnp.zeros_like(acc_c)
    bufs = ((w0, rt0, rf0), (w1, rt1, rf1))
    n = R // BI
    x, core = lax.axis_index("x"), lax.axis_index("core")

    def front(i, buf):
        r, rb = row_records(r_ref[pl.ds(pl.multiple_of(i * PK, PK), PK), :])
        buf[1][...] = rb.T
        buf[2][...] = r
        return rb

    def weights(rb, j, buf):
        e = jnp.dot(rb, ce[:, j:j + BJ], preferred_element_type=f32)
        m = jnp.dot(rb, cm[:, j:j + BJ], preferred_element_type=f32)
        buf[0][:, j:j + BJ] = (jnp.exp(e) * m).astype(bf16)

    def columns(j, buf):
        acc_c[:, j:j + BJ] += jnp.dot(buf[1][...], buf[0][:, j:j + BJ], preferred_element_type=f32)

    def rows(i, buf):
        a = jnp.dot(buf[0][...], cn[...], preferred_element_type=f32)
        t = a[:, :F] - a[:, NORM:NORM + 1] * buf[2][:, :F]
        t = t.reshape(BI // PR, 2, PR // 2, F)
        t = jnp.concatenate([t[:, 0], t[:, 1]], axis=-1).reshape(BI // 2, 128)
        k = lax.rem(i - x + NX, NX)
        a, b = t[:BI // 4], t[BI // 4:]
        keep_ref[k] = jnp.where(core == 0, a, b)
        swap_ref[k] = jnp.where(core == 0, b, a).astype(bf16)

    def both(i, new, old):
        rb = front(i, new)
        for j in range(0, C, BJ):
            weights(rb, j, new)
            columns(j, old)
        rows(i - 1, old)

    rb = front(0, bufs[0])
    for j in range(0, C, BJ):
        weights(rb, j, bufs[0])

    def step(k, carry):
        both(2 * k + 1, bufs[1], bufs[0])
        both(2 * k + 2, bufs[0], bufs[1])
        return carry

    lax.fori_loop(0, (n - 2) // 2, step, 0)
    both(n - 1, bufs[1], bufs[0])
    for j in range(0, C, BJ):
        columns(j, bufs[1])
    rows(n - 1, bufs[1])

    u = acc_c[:F, :] - acc_c[ONES:ONES + 1, :] * ct[:F, :].astype(f32)

    for d in range(NY):
        col_ref[d, :64] = u[:, (2 * d) * 128:(2 * d + 1) * 128].astype(bf16)
        col_ref[d, 64:128] = u[:, (2 * d + 1) * 128:(2 * d + 2) * 128].astype(bf16)
        h = u[:, 2 * NY * 128 + d * 64:2 * NY * 128 + d * 64 + 64]
        col_ref[d, 128:] = jnp.concatenate([h[:32], h[32:]], axis=1).astype(bf16)


def add_kernel(keep_ref, swap_ref, own_ref, *out_refs):
    own_ref[...] = keep_ref[0] + swap_ref[0].astype(f32)
    for k in range(1, NX):
        out_refs[k - 1][...] = (keep_ref[k] + swap_ref[k].astype(f32)).astype(bf16)


def finish_rows(row_ref, out_ref):
    s = jnp.sum(row_ref[...].astype(f32), axis=0)
    out_ref[...] = jnp.concatenate([s[:, :F], s[:, F:]], axis=0)


def finish_cols(col_ref, out_ref):
    s = jnp.sum(col_ref[...].astype(f32), axis=0)
    half = jnp.concatenate([s[128:, :64], s[128:, 64:]], axis=0)
    out_ref[...] = jnp.concatenate([s[:64], s[64:128], half], axis=1)


def body(row_points, row_solves, col_points, col_probes):
    shape = jax.ShapeDtypeStruct
    rows, cols = pl.pallas_call(
        pack_kernel,
        out_shape=(shape((NZ, 24, 128), bf16), shape((NY, 240, 128), bf16)),
        in_specs=[VM] * 4,
        out_specs=(VM, VM),
    )(row_points, row_solves, col_points.T, col_probes.T)
    rows = lax.all_to_all(rows, Z, 0, 0, tiled=True)
    rows, cols = lax.optimization_barrier((rows, cols))
    cols = lax.all_to_all(cols, "y", 0, 0, tiled=True)
    rows = lax.all_gather(rows.reshape(NZ * 24, 128), ("x", "core"), axis=0, tiled=True)
    part = R // (2 * NX * NC)
    keep, swap, col_part = pl.pallas_call(
        main_kernel,
        out_shape=(shape((NX, part, 128), f32), shape((NX, part, 128), bf16), shape((NY, 160, 128), bf16)),
        in_specs=[VM, VM],
        out_specs=(VM, VM, VM),
        scratch_shapes=[
            pltpu.VMEM((128, C), f32),
            pltpu.VMEM((128, C), bf16),
            pltpu.VMEM((128, C), bf16),
            pltpu.VMEM((128, C), bf16),
            pltpu.VMEM((C, 128), bf16),
            pltpu.VMEM((BI, C), bf16),
            pltpu.VMEM((BI, C), bf16),
            pltpu.VMEM((128, BI), bf16),
            pltpu.VMEM((128, BI), bf16),
            pltpu.VMEM((BI, 128), f32),
            pltpu.VMEM((BI, 128), f32),
        ],
        compiler_params=pltpu.CompilerParams(vmem_limit_bytes=40 * 2**20),
    )(rows, cols)
    col_part = lax.all_to_all(col_part, "y", 0, 0, tiled=True)
    swap = lax.ppermute(swap, "core", [(0, 1), (1, 0)])
    parts = pl.pallas_call(
        add_kernel,
        out_shape=(shape((part, 128), f32),) + (shape((part, 128), bf16),) * (NX - 1),
        in_specs=[VM, VM],
        out_specs=(VM,) * NX,
        compiler_params=SMALL,
    )(keep, swap)
    row_part = parts[0]
    for k in range(1, NX):
        row_part = row_part + lax.ppermute(parts[k], "x", [(i, (i + k) % NX) for i in range(NX)]).astype(f32)
    row_part = row_part.astype(bf16).reshape(NZ, PR // 2, 128)
    row_part, col_part = lax.optimization_barrier((row_part, col_part))
    row_part = lax.all_to_all(row_part, Z, 0, 0, tiled=True)
    row_grad = pl.pallas_call(
        finish_rows,
        out_shape=shape((PR, F), f32),
        in_specs=[VM],
        out_specs=VM,
        compiler_params=SMALL,
    )(row_part)
    col_grad = pl.pallas_call(
        finish_cols,
        out_shape=shape((F, PC), f32),
        in_specs=[VM],
        out_specs=VM,
        compiler_params=SMALL,
    )(col_part)
    return row_grad, col_grad.T


def solution(mesh):
    rings = Mesh(mesh.devices.reshape(SIZES), NAMES)
    row = P(("y", "zh", "x", "zl", "core"), None)
    col = P(("x", "zl", "core", "y", "zh"), None)
    return jax.shard_map(
        body,
        mesh=rings,
        in_specs=(row, row, col, col),
        out_specs=(row, col),
        check_vma=False,
    )
```

```python
import jax
import jax.numpy as jnp
from jax import lax
from jax.experimental import pallas as pl
from jax.experimental.pallas import tpu as pltpu
from jax.sharding import Mesh, PartitionSpec as P

f32, bf16 = jnp.float32, jnp.bfloat16

NAMES = ("y", "zh", "x", "zl", "core")
SIZES = (8, 3, 4, 4, 2)
Z = ("zh", "zl")
NX, NY, NZ, NC = 4, 8, 12, 2
PR, PC, F, Q = 32, 320, 64, 32
R, C = PR * NX * NZ * NC, PC * NY
NORM, ONES = F + Q, F + Q + 3
BI, BJ = R // NX, 512
PK = BI * 3 // 4

VM = pl.BlockSpec(memory_space=pltpu.VMEM)
SMALL = pltpu.CompilerParams(vmem_limit_bytes=8 * 2**20)


def thirds(v):
    a = v.astype(bf16)
    v = v - a.astype(f32)
    b = v.astype(bf16)
    return a, b, (v - b.astype(f32)).astype(bf16)


def pack_kernel(rp_ref, rs_ref, cp_ref, cq_ref, row_ref, col_ref):
    r, s = rp_ref[...].astype(f32), rs_ref[...].astype(f32)
    rec = jnp.concatenate(
        [
            jnp.concatenate([r[:16], r[16:]], axis=1),
            jnp.concatenate([s[:8], s[8:16], s[16:24], s[24:]], axis=1),
        ],
        axis=0,
    ).astype(bf16)
    for k in range(NZ):
        row_ref[k] = rec
    c = jnp.concatenate([cp_ref[...].astype(f32), cq_ref[...].astype(f32) * (1.0 / Q)], axis=0)
    half = jnp.concatenate([c[:48, 256:], c[48:, 256:]], axis=1)
    piece = jnp.concatenate([c[:, :128], c[:, 128:256], half], axis=0).astype(bf16)
    for k in range(NY):
        col_ref[k] = piece


def column_records(p_ref, ct, ce, cm, cn):
    for d in range(0, NY, 2):
        for e in (d, d + 1):
            ct[:96, (2 * e) * 128:(2 * e + 1) * 128] = p_ref[e, :96]
            ct[:96, (2 * e + 1) * 128:(2 * e + 2) * 128] = p_ref[e, 96:192]
        a, b = p_ref[d, 192:240], p_ref[d + 1, 192:240]
        at = (2 * NY + d // 2) * 128
        ct[:48, at:at + 128] = jnp.concatenate([a[:, :64], b[:, :64]], axis=1)
        ct[48:96, at:at + 128] = jnp.concatenate([a[:, 64:], b[:, 64:]], axis=1)
    wide = ct[:F, :].astype(f32)
    n = -0.5 * jnp.sum(wide * wide, axis=0, keepdims=True)
    ct[96:128, :] = jnp.concatenate(
        [jnp.ones((3, C), f32)] + [p.astype(f32) for p in thirds(n)] + [jnp.zeros((26, C), f32)], axis=0
    ).astype(bf16)
    ce[...] = ct[...]
    ce[F:F + Q, :] = jnp.zeros((Q, C), bf16)
    cm[...] = jnp.zeros_like(cm)
    cm[F:F + Q, :] = ct[F:F + Q, :]
    cn[...] = ce[...].T


def row_records(packed):
    n = packed.shape[0] // 24
    rec = packed.astype(f32).reshape(n, 24, 128)
    points, solves = rec[:, :16], rec[:, 16:]

    def roll(x, k):
        return pltpu.roll(x.reshape(-1, 128), k, 1).reshape(x.shape)

    r = jnp.stack([points, roll(points, 64)], axis=1).reshape(n * PR, 128)
    s = jnp.stack([roll(solves, 64), roll(solves, 32), solves, roll(solves, 96)], axis=1).reshape(n * PR, 128)
    lane = lax.broadcasted_iota(jnp.int32, (n * PR, 128), 1)
    r = jnp.where(lane < F, r, 0.0)
    a, b, c = [t.astype(f32) for t in thirds(-0.5 * jnp.sum(r * r, axis=1, keepdims=True))]
    ext = jnp.where(lane < ONES + 3, 1.0, 0.0)
    ext = jnp.where(lane == NORM, a, jnp.where(lane == NORM + 1, b, jnp.where(lane == NORM + 2, c, ext)))
    return r, jnp.where(lane < F, r, jnp.where(lane < NORM, s, ext)).astype(bf16)


def main_kernel(r_ref, p_ref, keep_ref, swap_ref, col_ref, acc_c, ct, ce, cm, cn, w0, w1, rt0, rt1, rf0, rf1):
    column_records(p_ref, ct, ce, cm, cn)
    acc_c[...] = jnp.zeros_like(acc_c)
    bufs = ((w0, rt0, rf0), (w1, rt1, rf1))
    n = R // BI
    x, core = lax.axis_index("x"), lax.axis_index("core")

    def front(i, buf):
        r, rb = row_records(r_ref[pl.ds(pl.multiple_of(i * PK, PK), PK), :])
        buf[1][...] = rb.T
        buf[2][...] = r
        return rb

    def weights(rb, j, buf):
        e = jnp.dot(rb, ce[:, j:j + BJ], preferred_element_type=f32)
        m = jnp.dot(rb, cm[:, j:j + BJ], preferred_element_type=f32)
        buf[0][:, j:j + BJ] = (jnp.exp(e) * m).astype(bf16)

    def columns(j, buf):
        acc_c[:, j:j + BJ] += jnp.dot(buf[1][...], buf[0][:, j:j + BJ], preferred_element_type=f32)

    def rows(i, buf):
        a = jnp.dot(buf[0][...], cn[...], preferred_element_type=f32)
        t = a[:, :F] - a[:, NORM:NORM + 1] * buf[2][:, :F]
        t = t.reshape(BI // PR, 2, PR // 2, F)
        t = jnp.concatenate([t[:, 0], t[:, 1]], axis=-1).reshape(BI // 2, 128)
        d = lax.bitwise_xor(jnp.int32(i), jnp.int32(x))
        k = jnp.where(d == 0, 0, jnp.where(d == 3, 1, d + 1))
        a, b = t[:BI // 4], t[BI // 4:]
        keep_ref[k] = jnp.where(core == 0, a, b)
        swap_ref[k] = jnp.where(core == 0, b, a).astype(bf16)

    def both(i, new, old):
        rb = front(i, new)
        for j in range(0, C, BJ):
            weights(rb, j, new)
            columns(j, old)
        rows(i - 1, old)

    rb = front(0, bufs[0])
    for j in range(0, C, BJ):
        weights(rb, j, bufs[0])

    def step(k, carry):
        both(2 * k + 1, bufs[1], bufs[0])
        both(2 * k + 2, bufs[0], bufs[1])
        return carry

    lax.fori_loop(0, (n - 2) // 2, step, 0)
    both(n - 1, bufs[1], bufs[0])
    for j in range(0, C, BJ):
        columns(j, bufs[1])
    rows(n - 1, bufs[1])

    u = acc_c[:F, :] - acc_c[ONES:ONES + 1, :] * ct[:F, :].astype(f32)

    for d in range(NY):
        col_ref[d, :64] = u[:, (2 * d) * 128:(2 * d + 1) * 128].astype(bf16)
        col_ref[d, 64:128] = u[:, (2 * d + 1) * 128:(2 * d + 2) * 128].astype(bf16)
        h = u[:, 2 * NY * 128 + d * 64:2 * NY * 128 + d * 64 + 64]
        col_ref[d, 128:] = jnp.concatenate([h[:32], h[32:]], axis=1).astype(bf16)


def add_kernel(keep_ref, got_ref, own_ref, out_ref):
    half = keep_ref.shape[0] // 2
    s = keep_ref[...] + got_ref[...].astype(f32)
    own_ref[...] = s[:half]
    out_ref[...] = s[half:].astype(bf16)


def add(keep, got):
    half = (keep.shape[0] // 2,) + keep.shape[1:]
    return pl.pallas_call(
        add_kernel,
        out_shape=(jax.ShapeDtypeStruct(half, f32), jax.ShapeDtypeStruct(half, bf16)),
        in_specs=[VM, VM],
        out_specs=(VM, VM),
        compiler_params=SMALL,
    )(keep, got)


def finish_rows(row_ref, out_ref):
    s = jnp.sum(row_ref[...].astype(f32), axis=0)
    out_ref[...] = jnp.concatenate([s[:, :F], s[:, F:]], axis=0)


def finish_cols(col_ref, out_ref):
    s = jnp.sum(col_ref[...].astype(f32), axis=0)
    half = jnp.concatenate([s[128:, :64], s[128:, 64:]], axis=0)
    out_ref[...] = jnp.concatenate([s[:64], s[64:128], half], axis=1)


def body(row_points, row_solves, col_points, col_probes):
    shape = jax.ShapeDtypeStruct
    rows, cols = pl.pallas_call(
        pack_kernel,
        out_shape=(shape((NZ, 24, 128), bf16), shape((NY, 240, 128), bf16)),
        in_specs=[VM] * 4,
        out_specs=(VM, VM),
    )(row_points, row_solves, col_points.T, col_probes.T)
    rows = lax.all_to_all(rows, Z, 0, 0, tiled=True)
    rows, cols = lax.optimization_barrier((rows, cols))
    cols = lax.all_to_all(cols, "y", 0, 0, tiled=True)
    rows = lax.all_gather(rows.reshape(NZ * 24, 128), ("x", "core"), axis=0, tiled=True)
    part = R // (2 * NX * NC)
    keep, swap, col_part = pl.pallas_call(
        main_kernel,
        out_shape=(shape((NX, part, 128), f32), shape((NX, part, 128), bf16), shape((NY, 160, 128), bf16)),
        in_specs=[VM, VM],
        out_specs=(VM, VM, VM),
        scratch_shapes=[
            pltpu.VMEM((128, C), f32),
            pltpu.VMEM((128, C), bf16),
            pltpu.VMEM((128, C), bf16),
            pltpu.VMEM((128, C), bf16),
            pltpu.VMEM((C, 128), bf16),
            pltpu.VMEM((BI, C), bf16),
            pltpu.VMEM((BI, C), bf16),
            pltpu.VMEM((128, BI), bf16),
            pltpu.VMEM((128, BI), bf16),
            pltpu.VMEM((BI, 128), f32),
            pltpu.VMEM((BI, 128), f32),
        ],
        compiler_params=pltpu.CompilerParams(vmem_limit_bytes=40 * 2**20),
    )(rows, cols)
    col_part = lax.all_to_all(col_part, "y", 0, 0, tiled=True)
    swap = lax.ppermute(swap, "core", [(0, 1), (1, 0)])
    keep, out = add(keep, swap)
    keep, out = add(keep, lax.ppermute(out, "x", [(0, 1), (1, 0), (2, 3), (3, 2)]))
    row_part = keep + lax.ppermute(out, "x", [(0, 3), (3, 0), (1, 2), (2, 1)]).astype(f32)
    row_part = row_part.astype(bf16).reshape(NZ, PR // 2, 128)
    row_part, col_part = lax.optimization_barrier((row_part, col_part))
    row_part = lax.all_to_all(row_part, Z, 0, 0, tiled=True)
    row_grad = pl.pallas_call(
        finish_rows,
        out_shape=shape((PR, F), f32),
        in_specs=[VM],
        out_specs=VM,
        compiler_params=SMALL,
    )(row_part)
    col_grad = pl.pallas_call(
        finish_cols,
        out_shape=shape((F, PC), f32),
        in_specs=[VM],
        out_specs=VM,
        compiler_params=SMALL,
    )(col_part)
    return row_grad, col_grad.T


def solution(mesh):
    rings = Mesh(mesh.devices.reshape(SIZES), NAMES)
    row = P(("y", "zh", "x", "zl", "core"), None)
    col = P(("x", "zl", "core", "y", "zh"), None)
    return jax.shard_map(
        body,
        mesh=rings,
        in_specs=(row, row, col, col),
        out_specs=(row, col),
        check_vma=False,
    )
```

```python
import jax
import jax.numpy as jnp
from jax import lax
from jax.experimental import pallas as pl
from jax.experimental.pallas import tpu as pltpu
from jax.sharding import Mesh, PartitionSpec as P

f32, bf16 = jnp.float32, jnp.bfloat16

NAMES = ("y", "zh", "x", "zl", "core")
SIZES = (8, 3, 4, 4, 2)
Z = ("zh", "zl")
NX, NY, NZ, NC = 4, 8, 12, 2
PR, PC, F, Q = 32, 320, 64, 32
R, C = PR * NX * NZ * NC, PC * NY
NORM, ONES = F + Q, F + Q + 3
BI, BJ = R // NX, 512
PK = BI * 3 // 4

VM = pl.BlockSpec(memory_space=pltpu.VMEM)
SMALL = pltpu.CompilerParams(vmem_limit_bytes=8 * 2**20)


def thirds(v):
    a = v.astype(bf16)
    v = v - a.astype(f32)
    b = v.astype(bf16)
    return a, b, (v - b.astype(f32)).astype(bf16)


def pack_rows(rp_ref, rs_ref, row_ref):
    r, s = rp_ref[...].astype(f32), rs_ref[...].astype(f32)
    rec = jnp.concatenate(
        [
            jnp.concatenate([r[:16], r[16:]], axis=1),
            jnp.concatenate([s[:8], s[8:16], s[16:24], s[24:]], axis=1),
        ],
        axis=0,
    ).astype(bf16)
    for k in range(NZ):
        row_ref[k] = rec


def pack_cols(cp_ref, cq_ref, col_ref):
    c = jnp.concatenate([cp_ref[...].astype(f32), cq_ref[...].astype(f32) * (1.0 / Q)], axis=0)
    half = jnp.concatenate([c[:48, 256:], c[48:, 256:]], axis=1)
    piece = jnp.concatenate([c[:, :128], c[:, 128:256], half], axis=0).astype(bf16)
    for k in range(NY):
        col_ref[k] = piece


def column_records(p_ref, ct, ce, cm, cn):
    for d in range(0, NY, 2):
        for e in (d, d + 1):
            ct[:96, (2 * e) * 128:(2 * e + 1) * 128] = p_ref[e, :96]
            ct[:96, (2 * e + 1) * 128:(2 * e + 2) * 128] = p_ref[e, 96:192]
        a, b = p_ref[d, 192:240], p_ref[d + 1, 192:240]
        at = (2 * NY + d // 2) * 128
        ct[:48, at:at + 128] = jnp.concatenate([a[:, :64], b[:, :64]], axis=1)
        ct[48:96, at:at + 128] = jnp.concatenate([a[:, 64:], b[:, 64:]], axis=1)
    wide = ct[:F, :].astype(f32)
    n = -0.5 * jnp.sum(wide * wide, axis=0, keepdims=True)
    ct[96:128, :] = jnp.concatenate(
        [jnp.ones((3, C), f32)] + [p.astype(f32) for p in thirds(n)] + [jnp.zeros((26, C), f32)], axis=0
    ).astype(bf16)
    ce[...] = ct[...]
    ce[F:F + Q, :] = jnp.zeros((Q, C), bf16)
    cm[...] = jnp.zeros_like(cm)
    cm[F:F + Q, :] = ct[F:F + Q, :]
    cn[...] = ce[...].T


def row_records(packed):
    n = packed.shape[0] // 24
    rec = packed.astype(f32).reshape(n, 24, 128)
    points, solves = rec[:, :16], rec[:, 16:]

    def roll(x, k):
        return pltpu.roll(x.reshape(-1, 128), k, 1).reshape(x.shape)

    r = jnp.stack([points, roll(points, 64)], axis=1).reshape(n * PR, 128)
    s = jnp.stack([roll(solves, 64), roll(solves, 32), solves, roll(solves, 96)], axis=1).reshape(n * PR, 128)
    lane = lax.broadcasted_iota(jnp.int32, (n * PR, 128), 1)
    r = jnp.where(lane < F, r, 0.0)
    a, b, c = [t.astype(f32) for t in thirds(-0.5 * jnp.sum(r * r, axis=1, keepdims=True))]
    ext = jnp.where(lane < ONES + 3, 1.0, 0.0)
    ext = jnp.where(lane == NORM, a, jnp.where(lane == NORM + 1, b, jnp.where(lane == NORM + 2, c, ext)))
    return r, jnp.where(lane < F, r, jnp.where(lane < NORM, s, ext)).astype(bf16)


def main_kernel(r_ref, p_ref, keep_ref, swap_ref, col_ref, acc_c, ct, ce, cm, cn, w0, w1, rt0, rt1, rf0, rf1):
    column_records(p_ref, ct, ce, cm, cn)
    acc_c[...] = jnp.zeros_like(acc_c)
    bufs = ((w0, rt0, rf0), (w1, rt1, rf1))
    n = R // BI
    x, core = lax.axis_index("x"), lax.axis_index("core")

    def front(i, buf):
        r, rb = row_records(r_ref[pl.ds(pl.multiple_of(i * PK, PK), PK), :])
        buf[1][...] = rb.T
        buf[2][...] = r
        return rb

    def weights(rb, j, buf):
        e = jnp.dot(rb, ce[:, j:j + BJ], preferred_element_type=f32)
        m = jnp.dot(rb, cm[:, j:j + BJ], preferred_element_type=f32)
        buf[0][:, j:j + BJ] = (jnp.exp(e) * m).astype(bf16)

    def columns(j, buf):
        acc_c[:, j:j + BJ] += jnp.dot(buf[1][...], buf[0][:, j:j + BJ], preferred_element_type=f32)

    def rows(i, buf):
        a = jnp.dot(buf[0][...], cn[...], preferred_element_type=f32)
        t = a[:, :F] - a[:, NORM:NORM + 1] * buf[2][:, :F]
        t = t.reshape(BI // PR, 2, PR // 2, F)
        t = jnp.concatenate([t[:, 0], t[:, 1]], axis=-1).reshape(BI // 2, 128)
        d = lax.bitwise_xor(jnp.int32(i), jnp.int32(x))
        k = jnp.where(d == 0, 0, jnp.where(d == 3, 1, d + 1))
        a, b = t[:BI // 4], t[BI // 4:]
        keep_ref[k] = jnp.where(core == 0, a, b)
        swap_ref[k] = jnp.where(core == 0, b, a).astype(bf16)

    def both(i, new, old):
        rb = front(i, new)
        for j in range(0, C, BJ):
            weights(rb, j, new)
            columns(j, old)
        rows(i - 1, old)

    rb = front(0, bufs[0])
    for j in range(0, C, BJ):
        weights(rb, j, bufs[0])

    def step(k, carry):
        both(2 * k + 1, bufs[1], bufs[0])
        both(2 * k + 2, bufs[0], bufs[1])
        return carry

    lax.fori_loop(0, (n - 2) // 2, step, 0)
    both(n - 1, bufs[1], bufs[0])
    for j in range(0, C, BJ):
        columns(j, bufs[1])
    rows(n - 1, bufs[1])

    u = acc_c[:F, :] - acc_c[ONES:ONES + 1, :] * ct[:F, :].astype(f32)

    for d in range(NY):
        col_ref[d, :64] = u[:, (2 * d) * 128:(2 * d + 1) * 128].astype(bf16)
        col_ref[d, 64:128] = u[:, (2 * d + 1) * 128:(2 * d + 2) * 128].astype(bf16)
        h = u[:, 2 * NY * 128 + d * 64:2 * NY * 128 + d * 64 + 64]
        col_ref[d, 128:] = jnp.concatenate([h[:32], h[32:]], axis=1).astype(bf16)


def add_kernel(keep_ref, got_ref, own_ref, out_ref):
    half = keep_ref.shape[0] // 2
    s = keep_ref[...] + got_ref[...].astype(f32)
    own_ref[...] = s[:half]
    out_ref[...] = s[half:].astype(bf16)


def add(keep, got):
    half = (keep.shape[0] // 2,) + keep.shape[1:]
    return pl.pallas_call(
        add_kernel,
        out_shape=(jax.ShapeDtypeStruct(half, f32), jax.ShapeDtypeStruct(half, bf16)),
        in_specs=[VM, VM],
        out_specs=(VM, VM),
        compiler_params=SMALL,
    )(keep, got)


def finish_rows(row_ref, out_ref):
    s = jnp.sum(row_ref[...].astype(f32), axis=0)
    out_ref[...] = jnp.concatenate([s[:, :F], s[:, F:]], axis=0)


def finish_cols(col_ref, out_ref):
    s = jnp.sum(col_ref[...].astype(f32), axis=0)
    half = jnp.concatenate([s[128:, :64], s[128:, 64:]], axis=0)
    out_ref[...] = jnp.concatenate([s[:64], s[64:128], half], axis=1)


def body(row_points, row_solves, col_points, col_probes):
    shape = jax.ShapeDtypeStruct
    rows = pl.pallas_call(
        pack_rows,
        out_shape=shape((NZ, 24, 128), bf16),
        in_specs=[VM] * 2,
        out_specs=VM,
    )(row_points, row_solves)
    cols = pl.pallas_call(
        pack_cols,
        out_shape=shape((NY, 240, 128), bf16),
        in_specs=[VM] * 2,
        out_specs=VM,
    )(col_points.T, col_probes.T)
    rows = lax.all_to_all(rows, Z, 0, 0, tiled=True)
    rows, cols = lax.optimization_barrier((rows, cols))
    cols = lax.all_to_all(cols, "y", 0, 0, tiled=True)
    rows = lax.all_gather(rows.reshape(NZ * 24, 128), ("x", "core"), axis=0, tiled=True)
    part = R // (2 * NX * NC)
    keep, swap, col_part = pl.pallas_call(
        main_kernel,
        out_shape=(shape((NX, part, 128), f32), shape((NX, part, 128), bf16), shape((NY, 160, 128), bf16)),
        in_specs=[VM, VM],
        out_specs=(VM, VM, VM),
        scratch_shapes=[
            pltpu.VMEM((128, C), f32),
            pltpu.VMEM((128, C), bf16),
            pltpu.VMEM((128, C), bf16),
            pltpu.VMEM((128, C), bf16),
            pltpu.VMEM((C, 128), bf16),
            pltpu.VMEM((BI, C), bf16),
            pltpu.VMEM((BI, C), bf16),
            pltpu.VMEM((128, BI), bf16),
            pltpu.VMEM((128, BI), bf16),
            pltpu.VMEM((BI, 128), f32),
            pltpu.VMEM((BI, 128), f32),
        ],
        compiler_params=pltpu.CompilerParams(vmem_limit_bytes=40 * 2**20),
    )(rows, cols)
    col_part = lax.all_to_all(col_part, "y", 0, 0, tiled=True)
    keep, out = add(keep, lax.ppermute(swap, "core", [(0, 1), (1, 0)]))
    keep, out = add(keep, lax.ppermute(out, "x", [(0, 1), (1, 0), (2, 3), (3, 2)]))
    row_part = keep + lax.ppermute(out, "x", [(0, 3), (3, 0), (1, 2), (2, 1)]).astype(f32)
    row_part = row_part.astype(bf16).reshape(NZ, PR // 2, 128)
    row_part, col_part = lax.optimization_barrier((row_part, col_part))
    row_part = lax.all_to_all(row_part, Z, 0, 0, tiled=True)
    row_grad = pl.pallas_call(
        finish_rows,
        out_shape=shape((PR, F), f32),
        in_specs=[VM],
        out_specs=VM,
        compiler_params=SMALL,
    )(row_part)
    col_grad = pl.pallas_call(
        finish_cols,
        out_shape=shape((F, PC), f32),
        in_specs=[VM],
        out_specs=VM,
        compiler_params=SMALL,
    )(col_part)
    return row_grad, col_grad.T


def solution(mesh):
    rings = Mesh(mesh.devices.reshape(SIZES), NAMES)
    row = P(("y", "zh", "x", "zl", "core"), None)
    col = P(("x", "zl", "core", "y", "zh"), None)
    return jax.shard_map(
        body,
        mesh=rings,
        in_specs=(row, row, col, col),
        out_specs=(row, col),
        check_vma=False,
    )
```

```python
import jax
import jax.numpy as jnp
from jax import lax
from jax.experimental import pallas as pl
from jax.experimental.pallas import tpu as pltpu
from jax.sharding import Mesh, PartitionSpec as P

f32, bf16 = jnp.float32, jnp.bfloat16

NAMES = ("y", "zh", "xa", "xb", "zl", "core")
SIZES = (8, 3, 2, 2, 4, 2)
XZ = ("xa", "zh", "zl")
ORDER = [[0, 2, 4, 6, 1, 3, 5, 7]]
NX, NY, NZ, NC = 4, 8, 12, 2
PR, PC, F, Q = 32, 320, 64, 32
R, C = PR * NX * NZ * NC, PC * NY
NORM, ONES = F + Q, F + Q + 3
BI, BJ = R // NX, 512
PK = BI * 3 // 4

VM = pl.BlockSpec(memory_space=pltpu.VMEM)
SMALL = pltpu.CompilerParams(vmem_limit_bytes=8 * 2**20)


def thirds(v):
    a = v.astype(bf16)
    v = v - a.astype(f32)
    b = v.astype(bf16)
    return a, b, (v - b.astype(f32)).astype(bf16)


def pack_rows(rp_ref, rs_ref, row_ref):
    r, s = rp_ref[...].astype(f32), rs_ref[...].astype(f32)
    rec = jnp.concatenate(
        [
            jnp.concatenate([r[:16], r[16:]], axis=1),
            jnp.concatenate([s[:8], s[8:16], s[16:24], s[24:]], axis=1),
        ],
        axis=0,
    ).astype(bf16)
    for k in range(2 * NZ):
        row_ref[k] = rec


def pack_cols(cp_ref, cq_ref, col_ref):
    c = jnp.concatenate([cp_ref[...].astype(f32), cq_ref[...].astype(f32) * (1.0 / Q)], axis=0)
    half = jnp.concatenate([c[:48, 256:], c[48:, 256:]], axis=1)
    piece = jnp.concatenate([c[:, :128], c[:, 128:256], half], axis=0).astype(bf16)
    for k in range(NY):
        col_ref[k] = piece


def column_records(p_ref, ct, ce, cm, cn):
    for d in range(0, NY, 2):
        for e in (d, d + 1):
            ct[:96, (2 * e) * 128:(2 * e + 1) * 128] = p_ref[e, :96]
            ct[:96, (2 * e + 1) * 128:(2 * e + 2) * 128] = p_ref[e, 96:192]
        a, b = p_ref[d, 192:240], p_ref[d + 1, 192:240]
        at = (2 * NY + d // 2) * 128
        ct[:48, at:at + 128] = jnp.concatenate([a[:, :64], b[:, :64]], axis=1)
        ct[48:96, at:at + 128] = jnp.concatenate([a[:, 64:], b[:, 64:]], axis=1)
    wide = ct[:F, :].astype(f32)
    n = -0.5 * jnp.sum(wide * wide, axis=0, keepdims=True)
    ct[96:128, :] = jnp.concatenate(
        [jnp.ones((3, C), f32)] + [p.astype(f32) for p in thirds(n)] + [jnp.zeros((26, C), f32)], axis=0
    ).astype(bf16)
    ce[...] = ct[...]
    ce[F:F + Q, :] = jnp.zeros((Q, C), bf16)
    cm[...] = jnp.zeros_like(cm)
    cm[F:F + Q, :] = ct[F:F + Q, :]
    cn[...] = ce[...].T


def row_records(packed):
    n = packed.shape[0] // 24
    rec = packed.astype(f32).reshape(n, 24, 128)
    points, solves = rec[:, :16], rec[:, 16:]

    def roll(x, k):
        return pltpu.roll(x.reshape(-1, 128), k, 1).reshape(x.shape)

    r = jnp.stack([points, roll(points, 64)], axis=1).reshape(n * PR, 128)
    s = jnp.stack([roll(solves, 64), roll(solves, 32), solves, roll(solves, 96)], axis=1).reshape(n * PR, 128)
    lane = lax.broadcasted_iota(jnp.int32, (n * PR, 128), 1)
    r = jnp.where(lane < F, r, 0.0)
    a, b, c = [t.astype(f32) for t in thirds(-0.5 * jnp.sum(r * r, axis=1, keepdims=True))]
    ext = jnp.where(lane < ONES + 3, 1.0, 0.0)
    ext = jnp.where(lane == NORM, a, jnp.where(lane == NORM + 1, b, jnp.where(lane == NORM + 2, c, ext)))
    return r, jnp.where(lane < F, r, jnp.where(lane < NORM, s, ext)).astype(bf16)


def main_kernel(r_ref, p_ref, keep_ref, swap_ref, col_ref, acc_c, ct, ce, cm, cn, w0, w1, rt0, rt1, rf0, rf1, part):
    column_records(p_ref, ct, ce, cm, cn)
    acc_c[...] = jnp.zeros_like(acc_c)
    bufs = ((w0, rt0, rf0), (w1, rt1, rf1))
    n = R // BI
    xb, core = lax.axis_index("xb"), lax.axis_index("core")

    def front(i, buf):
        r, rb = row_records(r_ref[pl.ds(pl.multiple_of(i * PK, PK), PK), :])
        buf[1][...] = rb.T
        buf[2][...] = r
        return rb

    def weights(rb, j, buf):
        e = jnp.dot(rb, ce[:, j:j + BJ], preferred_element_type=f32)
        m = jnp.dot(rb, cm[:, j:j + BJ], preferred_element_type=f32)
        buf[0][:, j:j + BJ] = (jnp.exp(e) * m).astype(bf16)

    def columns(j, buf):
        acc_c[:, j:j + BJ] += jnp.dot(buf[1][...], buf[0][:, j:j + BJ], preferred_element_type=f32)

    def rows(i, buf):
        a = jnp.dot(buf[0][...], cn[...], preferred_element_type=f32)
        t = a[:, :F] - a[:, NORM:NORM + 1] * buf[2][:, :F]
        t = t.reshape(BI // PR, 2, PR // 2, F)
        t = jnp.concatenate([t[:, 0], t[:, 1]], axis=-1).reshape(BI // 2, 128)
        at = 4 * jnp.int32(i % 2 != core) + 2 * jnp.int32(i // 2 != xb)
        for h in range(2):
            part[at + h] = t[h * (BI // 4):(h + 1) * (BI // 4)]

    def both(i, new, old):
        rb = front(i, new)
        for j in range(0, C, BJ):
            weights(rb, j, new)
            columns(j, old)
        rows(i - 1, old)

    rb = front(0, bufs[0])
    for j in range(0, C, BJ):
        weights(rb, j, bufs[0])

    def step(k, carry):
        both(2 * k + 1, bufs[1], bufs[0])
        both(2 * k + 2, bufs[0], bufs[1])
        return carry

    lax.fori_loop(0, (n - 2) // 2, step, 0)
    both(n - 1, bufs[1], bufs[0])
    for j in range(0, C, BJ):
        columns(j, bufs[1])
    rows(n - 1, bufs[1])

    keep_ref[...] = part[:4]
    swap_ref[...] = part[4:].astype(bf16)
    u = acc_c[:F, :] - acc_c[ONES:ONES + 1, :] * ct[:F, :].astype(f32)

    for d in range(NY):
        col_ref[d, :64] = u[:, (2 * d) * 128:(2 * d + 1) * 128].astype(bf16)
        col_ref[d, 64:128] = u[:, (2 * d + 1) * 128:(2 * d + 2) * 128].astype(bf16)
        h = u[:, 2 * NY * 128 + d * 64:2 * NY * 128 + d * 64 + 64]
        col_ref[d, 128:] = jnp.concatenate([h[:32], h[32:]], axis=1).astype(bf16)


def add_kernel(keep_ref, got_ref, own_ref, out_ref):
    half = keep_ref.shape[0] // 2
    s = keep_ref[...] + got_ref[...].astype(f32)
    own_ref[...] = s[:half]
    out_ref[...] = s[half:].astype(bf16)


def add(keep, got):
    half = (keep.shape[0] // 2,) + keep.shape[1:]
    return pl.pallas_call(
        add_kernel,
        out_shape=(jax.ShapeDtypeStruct(half, f32), jax.ShapeDtypeStruct(half, bf16)),
        in_specs=[VM, VM],
        out_specs=(VM, VM),
        compiler_params=SMALL,
    )(keep, got)


def finish_rows(row_ref, out_ref):
    s = jnp.sum(row_ref[...].astype(f32), axis=0)
    out_ref[...] = jnp.concatenate([s[:, :F], s[:, F:]], axis=0)


def finish_cols(col_ref, out_ref):
    s = jnp.sum(col_ref[...].astype(f32), axis=0)
    half = jnp.concatenate([s[128:, :64], s[128:, 64:]], axis=0)
    out_ref[...] = jnp.concatenate([s[:64], s[64:128], half], axis=1)


def body(row_points, row_solves, col_points, col_probes):
    shape = jax.ShapeDtypeStruct
    rows = pl.pallas_call(
        pack_rows,
        out_shape=shape((2 * NZ, 24, 128), bf16),
        in_specs=[VM] * 2,
        out_specs=VM,
    )(row_points, row_solves)
    cols = pl.pallas_call(
        pack_cols,
        out_shape=shape((NY, 240, 128), bf16),
        in_specs=[VM] * 2,
        out_specs=VM,
    )(col_points.T, col_probes.T)
    rows = lax.all_to_all(rows, XZ, 0, 0, tiled=True)
    rows, cols = lax.optimization_barrier((rows, cols))
    cols = lax.all_to_all(cols, "y", 0, 0, tiled=True, axis_index_groups=ORDER)
    rows = lax.all_gather(rows.reshape(2 * NZ * 24, 128), ("xb", "core"), axis=0, tiled=True)
    part = R // (2 * NX * NC)
    keep, swap, col_part = pl.pallas_call(
        main_kernel,
        out_shape=(shape((NX, part, 128), f32), shape((NX, part, 128), bf16), shape((NY, 160, 128), bf16)),
        in_specs=[VM, VM],
        out_specs=(VM, VM, VM),
        scratch_shapes=[
            pltpu.VMEM((128, C), f32),
            pltpu.VMEM((128, C), bf16),
            pltpu.VMEM((128, C), bf16),
            pltpu.VMEM((128, C), bf16),
            pltpu.VMEM((C, 128), bf16),
            pltpu.VMEM((BI, C), bf16),
            pltpu.VMEM((BI, C), bf16),
            pltpu.VMEM((128, BI), bf16),
            pltpu.VMEM((128, BI), bf16),
            pltpu.VMEM((BI, 128), f32),
            pltpu.VMEM((BI, 128), f32),
            pltpu.VMEM((2 * NX, part, 128), f32),
        ],
        compiler_params=pltpu.CompilerParams(vmem_limit_bytes=40 * 2**20),
    )(rows, cols)
    col_part = lax.all_to_all(col_part, "y", 0, 0, tiled=True, axis_index_groups=ORDER)
    keep, out = add(keep, lax.ppermute(swap, "core", [(0, 1), (1, 0)]))
    row_part = keep + lax.ppermute(out, "xb", [(0, 1), (1, 0)]).astype(f32)
    row_part = row_part.astype(bf16).reshape(2 * NZ, PR // 2, 128)
    row_part, col_part = lax.optimization_barrier((row_part, col_part))
    row_part = lax.all_to_all(row_part, XZ, 0, 0, tiled=True)
    row_grad = pl.pallas_call(
        finish_rows,
        out_shape=shape((PR, F), f32),
        in_specs=[VM],
        out_specs=VM,
        compiler_params=SMALL,
    )(row_part)
    col_grad = pl.pallas_call(
        finish_cols,
        out_shape=shape((F, PC), f32),
        in_specs=[VM],
        out_specs=VM,
        compiler_params=SMALL,
    )(col_part)
    return row_grad, col_grad.T


def solution(mesh):
    rings = Mesh(mesh.devices.reshape(SIZES), NAMES)
    row = P(("y", "zh", "xa", "xb", "zl", "core"), None)
    col = P(("xa", "xb", "zl", "core", "y", "zh"), None)
    return jax.shard_map(
        body,
        mesh=rings,
        in_specs=(row, row, col, col),
        out_specs=(row, col),
        check_vma=False,
    )
```

```python
import jax
import jax.numpy as jnp
from jax import lax
from jax.experimental import pallas as pl
from jax.experimental.pallas import tpu as pltpu
from jax.sharding import Mesh, PartitionSpec as P

f32, bf16 = jnp.float32, jnp.bfloat16

NAMES = ("y", "zh", "xa", "xb", "zl", "core")
SIZES = (8, 3, 2, 2, 4, 2)
XZ = ("xa", "zh", "zl")
ORDER = [[0, 2, 4, 6, 1, 3, 5, 7]]
NX, NY, NZ, NC = 4, 8, 12, 2
PR, PC, F, Q = 32, 320, 64, 32
R, C = PR * NX * NZ * NC, PC * NY
NORM, ONES = F + Q, F + Q + 3
BI, BJ = R // NX, 512
PK = BI * 3 // 4

VM = pl.BlockSpec(memory_space=pltpu.VMEM)
SMALL = pltpu.CompilerParams(vmem_limit_bytes=8 * 2**20)


def thirds(v):
    a = v.astype(bf16)
    v = v - a.astype(f32)
    b = v.astype(bf16)
    return a, b, (v - b.astype(f32)).astype(bf16)


def pack_rows(rp_ref, rs_ref, row_ref):
    r, s = rp_ref[...].astype(f32), rs_ref[...].astype(f32)
    rec = jnp.concatenate(
        [
            jnp.concatenate([r[:16], r[16:]], axis=1),
            jnp.concatenate([s[:8], s[8:16], s[16:24], s[24:]], axis=1),
        ],
        axis=0,
    ).astype(bf16)
    for k in range(NZ):
        row_ref[k] = rec


def pack_cols(cp_ref, cq_ref, col_ref):
    c = jnp.concatenate([cp_ref[...].astype(f32), cq_ref[...].astype(f32) * (1.0 / Q)], axis=0)
    half = jnp.concatenate([c[:48, 256:], c[48:, 256:]], axis=1)
    piece = jnp.concatenate([c[:, :128], c[:, 128:256], half], axis=0).astype(bf16)
    for k in range(NY):
        col_ref[k] = piece


def column_records(p_ref, ct, ce, cm, cn):
    for d in range(0, NY, 2):
        for e in (d, d + 1):
            ct[:96, (2 * e) * 128:(2 * e + 1) * 128] = p_ref[e, :96]
            ct[:96, (2 * e + 1) * 128:(2 * e + 2) * 128] = p_ref[e, 96:192]
        a, b = p_ref[d, 192:240], p_ref[d + 1, 192:240]
        at = (2 * NY + d // 2) * 128
        ct[:48, at:at + 128] = jnp.concatenate([a[:, :64], b[:, :64]], axis=1)
        ct[48:96, at:at + 128] = jnp.concatenate([a[:, 64:], b[:, 64:]], axis=1)
    wide = ct[:F, :].astype(f32)
    n = -0.5 * jnp.sum(wide * wide, axis=0, keepdims=True)
    ct[96:128, :] = jnp.concatenate(
        [jnp.ones((3, C), f32)] + [p.astype(f32) for p in thirds(n)] + [jnp.zeros((26, C), f32)], axis=0
    ).astype(bf16)
    ce[...] = ct[...]
    ce[F:F + Q, :] = jnp.zeros((Q, C), bf16)
    cm[...] = jnp.zeros_like(cm)
    cm[F:F + Q, :] = ct[F:F + Q, :]
    cn[...] = ce[...].T


def row_records(packed):
    n = packed.shape[0] // 24
    rec = packed.astype(f32).reshape(n, 24, 128)
    points, solves = rec[:, :16], rec[:, 16:]

    def roll(x, k):
        return pltpu.roll(x.reshape(-1, 128), k, 1).reshape(x.shape)

    r = jnp.stack([points, roll(points, 64)], axis=1).reshape(n * PR, 128)
    s = jnp.stack([roll(solves, 64), roll(solves, 32), solves, roll(solves, 96)], axis=1).reshape(n * PR, 128)
    lane = lax.broadcasted_iota(jnp.int32, (n * PR, 128), 1)
    r = jnp.where(lane < F, r, 0.0)
    a, b, c = [t.astype(f32) for t in thirds(-0.5 * jnp.sum(r * r, axis=1, keepdims=True))]
    ext = jnp.where(lane < ONES + 3, 1.0, 0.0)
    ext = jnp.where(lane == NORM, a, jnp.where(lane == NORM + 1, b, jnp.where(lane == NORM + 2, c, ext)))
    return r, jnp.where(lane < F, r, jnp.where(lane < NORM, s, ext)).astype(bf16)


def main_kernel(r_ref, p_ref, keep_ref, swap_ref, col_ref, acc_c, ct, ce, cm, cn, w0, w1, rt0, rt1, rf0, rf1, part):
    column_records(p_ref, ct, ce, cm, cn)
    acc_c[...] = jnp.zeros_like(acc_c)
    bufs = ((w0, rt0, rf0), (w1, rt1, rf1))
    n = R // BI
    xb, core = lax.axis_index("xb"), lax.axis_index("core")

    def front(i, buf):
        r, rb = row_records(r_ref[pl.ds(pl.multiple_of(i * PK, PK), PK), :])
        buf[1][...] = rb.T
        buf[2][...] = r
        return rb

    def weights(rb, j, buf):
        e = jnp.dot(rb, ce[:, j:j + BJ], preferred_element_type=f32)
        m = jnp.dot(rb, cm[:, j:j + BJ], preferred_element_type=f32)
        buf[0][:, j:j + BJ] = (jnp.exp(e) * m).astype(bf16)

    def columns(j, buf):
        acc_c[:, j:j + BJ] += jnp.dot(buf[1][...], buf[0][:, j:j + BJ], preferred_element_type=f32)

    def rows(i, buf):
        a = jnp.dot(buf[0][...], cn[...], preferred_element_type=f32)
        t = a[:, :F] - a[:, NORM:NORM + 1] * buf[2][:, :F]
        t = t.reshape(BI // PR, 2, PR // 2, F)
        t = jnp.concatenate([t[:, 0], t[:, 1]], axis=-1).reshape(BI // 2, 128)
        at = 2 * jnp.int32(i % 2 != xb) + i // 2
        for h in range(2):
            part[at + 4 * jnp.int32(h != core)] = t[h * (BI // 4):(h + 1) * (BI // 4)]

    def both(i, new, old):
        rb = front(i, new)
        for j in range(0, C, BJ):
            weights(rb, j, new)
            columns(j, old)
        rows(i - 1, old)

    rb = front(0, bufs[0])
    for j in range(0, C, BJ):
        weights(rb, j, bufs[0])

    def step(k, carry):
        both(2 * k + 1, bufs[1], bufs[0])
        both(2 * k + 2, bufs[0], bufs[1])
        return carry

    lax.fori_loop(0, (n - 2) // 2, step, 0)
    both(n - 1, bufs[1], bufs[0])
    for j in range(0, C, BJ):
        columns(j, bufs[1])
    rows(n - 1, bufs[1])

    keep_ref[...] = part[:4]
    swap_ref[...] = part[4:].astype(bf16)
    u = acc_c[:F, :] - acc_c[ONES:ONES + 1, :] * ct[:F, :].astype(f32)

    for d in range(NY):
        col_ref[d, :64] = u[:, (2 * d) * 128:(2 * d + 1) * 128].astype(bf16)
        col_ref[d, 64:128] = u[:, (2 * d + 1) * 128:(2 * d + 2) * 128].astype(bf16)
        h = u[:, 2 * NY * 128 + d * 64:2 * NY * 128 + d * 64 + 64]
        col_ref[d, 128:] = jnp.concatenate([h[:32], h[32:]], axis=1).astype(bf16)


def add_kernel(keep_ref, got_ref, own_ref, out_ref):
    half = keep_ref.shape[0] // 2
    s = keep_ref[...] + got_ref[...].astype(f32)
    own_ref[...] = s[:half]
    out_ref[...] = s[half:].astype(bf16)


def add(keep, got):
    half = (keep.shape[0] // 2,) + keep.shape[1:]
    return pl.pallas_call(
        add_kernel,
        out_shape=(jax.ShapeDtypeStruct(half, f32), jax.ShapeDtypeStruct(half, bf16)),
        in_specs=[VM, VM],
        out_specs=(VM, VM),
        compiler_params=SMALL,
    )(keep, got)


def finish_rows(row_ref, out_ref):
    s = jnp.sum(row_ref[...].astype(f32), axis=0)
    out_ref[...] = jnp.concatenate([s[:, :F], s[:, F:]], axis=0)


def finish_cols(col_ref, out_ref):
    s = jnp.sum(col_ref[...].astype(f32), axis=0)
    half = jnp.concatenate([s[128:, :64], s[128:, 64:]], axis=0)
    out_ref[...] = jnp.concatenate([s[:64], s[64:128], half], axis=1)


def body(row_points, row_solves, col_points, col_probes):
    shape = jax.ShapeDtypeStruct
    rows = pl.pallas_call(
        pack_rows,
        out_shape=shape((NZ, 24, 128), bf16),
        in_specs=[VM] * 2,
        out_specs=VM,
    )(row_points, row_solves)
    cols = pl.pallas_call(
        pack_cols,
        out_shape=shape((NY, 240, 128), bf16),
        in_specs=[VM] * 2,
        out_specs=VM,
    )(col_points.T, col_probes.T)
    rows = lax.all_to_all(rows, ("zh", "zl"), 0, 0, tiled=True)
    rows, cols = lax.optimization_barrier((rows, cols))
    cols = lax.all_to_all(cols, "y", 0, 0, tiled=True, axis_index_groups=ORDER)
    rows = lax.all_gather(rows.reshape(NZ * 24, 128), ("xa", "xb", "core"), axis=0, tiled=True)
    part = R // (2 * NX * NC)
    keep, swap, col_part = pl.pallas_call(
        main_kernel,
        out_shape=(shape((NX, part, 128), f32), shape((NX, part, 128), bf16), shape((NY, 160, 128), bf16)),
        in_specs=[VM, VM],
        out_specs=(VM, VM, VM),
        scratch_shapes=[
            pltpu.VMEM((128, C), f32),
            pltpu.VMEM((128, C), bf16),
            pltpu.VMEM((128, C), bf16),
            pltpu.VMEM((128, C), bf16),
            pltpu.VMEM((C, 128), bf16),
            pltpu.VMEM((BI, C), bf16),
            pltpu.VMEM((BI, C), bf16),
            pltpu.VMEM((128, BI), bf16),
            pltpu.VMEM((128, BI), bf16),
            pltpu.VMEM((BI, 128), f32),
            pltpu.VMEM((BI, 128), f32),
            pltpu.VMEM((2 * NX, part, 128), f32),
        ],
        compiler_params=pltpu.CompilerParams(vmem_limit_bytes=40 * 2**20),
    )(rows, cols)
    col_part = lax.all_to_all(col_part, "y", 0, 0, tiled=True, axis_index_groups=ORDER)
    keep, out = add(keep, lax.ppermute(swap, "core", [(0, 1), (1, 0)]))
    row_part = keep + lax.ppermute(out, "xb", [(0, 1), (1, 0)]).astype(f32)
    row_part = row_part.astype(bf16).reshape(2 * NZ, PR // 2, 128)
    row_part, col_part = lax.optimization_barrier((row_part, col_part))
    row_part = lax.all_to_all(row_part, XZ, 0, 0, tiled=True)
    row_grad = pl.pallas_call(
        finish_rows,
        out_shape=shape((PR, F), f32),
        in_specs=[VM],
        out_specs=VM,
        compiler_params=SMALL,
    )(row_part)
    col_grad = pl.pallas_call(
        finish_cols,
        out_shape=shape((F, PC), f32),
        in_specs=[VM],
        out_specs=VM,
        compiler_params=SMALL,
    )(col_part)
    return row_grad, col_grad.T


def solution(mesh):
    rings = Mesh(mesh.devices.reshape(SIZES), NAMES)
    row = P(("y", "zh", "xa", "xb", "zl", "core"), None)
    col = P(("xa", "xb", "zl", "core", "y", "zh"), None)
    return jax.shard_map(
        body,
        mesh=rings,
        in_specs=(row, row, col, col),
        out_specs=(row, col),
        check_vma=False,
    )
```

```python
import jax
import jax.numpy as jnp
from jax import lax
from jax.experimental import pallas as pl
from jax.experimental.pallas import tpu as pltpu
from jax.sharding import Mesh, PartitionSpec as P

f32, bf16 = jnp.float32, jnp.bfloat16

NAMES = ("y", "zh", "xa", "xb", "zl", "core")
SIZES = (8, 3, 2, 2, 4, 2)
XZ = ("xa", "zh", "zl")
Y_ORDER = [0, 2, 4, 6, 1, 3, 5, 7]
Z_ORDER = [0, 2, 4, 6, 8, 10, 1, 3, 5, 7, 9, 11]
TURN = 3
XZ_ORDER = [12 * a + z for a in range(2) for z in Z_ORDER[TURN:] + Z_ORDER[:TURN]]
NX, NY, NZ, NC = 4, 8, 12, 2
PR, PC, F, Q = 32, 320, 64, 32
R, C = PR * NX * NZ * NC, PC * NY
NORM, ONES = F + Q, F + Q + 3
BI, BJ = R // NX, 512
PK = BI * 3 // 4

VM = pl.BlockSpec(memory_space=pltpu.VMEM)
SMALL = pltpu.CompilerParams(vmem_limit_bytes=8 * 2**20)


def thirds(v):
    a = v.astype(bf16)
    v = v - a.astype(f32)
    b = v.astype(bf16)
    return a, b, (v - b.astype(f32)).astype(bf16)


def pack_rows(rp_ref, rs_ref, row_ref):
    r, s = rp_ref[...].astype(f32), rs_ref[...].astype(f32)
    rec = jnp.concatenate(
        [
            jnp.concatenate([r[:16], r[16:]], axis=1),
            jnp.concatenate([s[:8], s[8:16], s[16:24], s[24:]], axis=1),
        ],
        axis=0,
    ).astype(bf16)
    for k in range(NZ):
        row_ref[k] = rec


def pack_cols(cp_ref, cq_ref, col_ref):
    c = jnp.concatenate([cp_ref[...].astype(f32), cq_ref[...].astype(f32) * (1.0 / Q)], axis=0)
    half = jnp.concatenate([c[:48, 256:], c[48:, 256:]], axis=1)
    piece = jnp.concatenate([c[:, :128], c[:, 128:256], half], axis=0).astype(bf16)
    for k in range(NY):
        col_ref[k] = piece


def column_records(p_ref, ct, ce, cm, cn):
    for d in range(0, NY, 2):
        for e in (d, d + 1):
            ct[:96, (2 * e) * 128:(2 * e + 1) * 128] = p_ref[e, :96]
            ct[:96, (2 * e + 1) * 128:(2 * e + 2) * 128] = p_ref[e, 96:192]
        a, b = p_ref[d, 192:240], p_ref[d + 1, 192:240]
        at = (2 * NY + d // 2) * 128
        ct[:48, at:at + 128] = jnp.concatenate([a[:, :64], b[:, :64]], axis=1)
        ct[48:96, at:at + 128] = jnp.concatenate([a[:, 64:], b[:, 64:]], axis=1)
    wide = ct[:F, :].astype(f32)
    n = -0.5 * jnp.sum(wide * wide, axis=0, keepdims=True)
    ct[96:128, :] = jnp.concatenate(
        [jnp.ones((3, C), f32)] + [p.astype(f32) for p in thirds(n)] + [jnp.zeros((26, C), f32)], axis=0
    ).astype(bf16)
    ce[...] = ct[...]
    ce[F:F + Q, :] = jnp.zeros((Q, C), bf16)
    cm[...] = jnp.zeros_like(cm)
    cm[F:F + Q, :] = ct[F:F + Q, :]
    cn[...] = ce[...].T


def row_records(packed):
    n = packed.shape[0] // 24
    rec = packed.astype(f32).reshape(n, 24, 128)
    points, solves = rec[:, :16], rec[:, 16:]

    def roll(x, k):
        return pltpu.roll(x.reshape(-1, 128), k, 1).reshape(x.shape)

    r = jnp.stack([points, roll(points, 64)], axis=1).reshape(n * PR, 128)
    s = jnp.stack([roll(solves, 64), roll(solves, 32), solves, roll(solves, 96)], axis=1).reshape(n * PR, 128)
    lane = lax.broadcasted_iota(jnp.int32, (n * PR, 128), 1)
    r = jnp.where(lane < F, r, 0.0)
    a, b, c = [t.astype(f32) for t in thirds(-0.5 * jnp.sum(r * r, axis=1, keepdims=True))]
    ext = jnp.where(lane < ONES + 3, 1.0, 0.0)
    ext = jnp.where(lane == NORM, a, jnp.where(lane == NORM + 1, b, jnp.where(lane == NORM + 2, c, ext)))
    return r, jnp.where(lane < F, r, jnp.where(lane < NORM, s, ext)).astype(bf16)


def main_kernel(r_ref, p_ref, keep_ref, swap_ref, col_ref, acc_c, ct, ce, cm, cn, w0, w1, rt0, rt1, rf0, rf1, part):
    column_records(p_ref, ct, ce, cm, cn)
    acc_c[...] = jnp.zeros_like(acc_c)
    bufs = ((w0, rt0, rf0), (w1, rt1, rf1))
    n = R // BI
    xb, core = lax.axis_index("xb"), lax.axis_index("core")

    def front(i, buf):
        r, rb = row_records(r_ref[pl.ds(pl.multiple_of(i * PK, PK), PK), :])
        buf[1][...] = rb.T
        buf[2][...] = r
        return rb

    def weights(rb, j, buf):
        e = jnp.dot(rb, ce[:, j:j + BJ], preferred_element_type=f32)
        m = jnp.dot(rb, cm[:, j:j + BJ], preferred_element_type=f32)
        buf[0][:, j:j + BJ] = (jnp.exp(e) * m).astype(bf16)

    def columns(j, buf):
        acc_c[:, j:j + BJ] += jnp.dot(buf[1][...], buf[0][:, j:j + BJ], preferred_element_type=f32)

    def rows(i, buf):
        a = jnp.dot(buf[0][...], cn[...], preferred_element_type=f32)
        t = a[:, :F] - a[:, NORM:NORM + 1] * buf[2][:, :F]
        t = t.reshape(BI // PR, 2, PR // 2, F)
        t = jnp.concatenate([t[:, 0], t[:, 1]], axis=-1).reshape(BI // 2, 128)
        at = 2 * jnp.int32(i % 2 != xb) + i // 2
        for h in range(2):
            part[at + 4 * jnp.int32(h != core)] = t[h * (BI // 4):(h + 1) * (BI // 4)]

    def both(i, new, old):
        rb = front(i, new)
        for j in range(0, C, BJ):
            weights(rb, j, new)
            columns(j, old)
        rows(i - 1, old)

    rb = front(0, bufs[0])
    for j in range(0, C, BJ):
        weights(rb, j, bufs[0])

    def step(k, carry):
        both(2 * k + 1, bufs[1], bufs[0])
        both(2 * k + 2, bufs[0], bufs[1])
        return carry

    lax.fori_loop(0, (n - 2) // 2, step, 0)
    both(n - 1, bufs[1], bufs[0])
    for j in range(0, C, BJ):
        columns(j, bufs[1])
    rows(n - 1, bufs[1])

    keep_ref[...] = part[:4]
    swap_ref[...] = part[4:].astype(bf16)
    u = acc_c[:F, :] - acc_c[ONES:ONES + 1, :] * ct[:F, :].astype(f32)

    for d in range(NY):
        col_ref[d, :64] = u[:, (2 * d) * 128:(2 * d + 1) * 128].astype(bf16)
        col_ref[d, 64:128] = u[:, (2 * d + 1) * 128:(2 * d + 2) * 128].astype(bf16)
        h = u[:, 2 * NY * 128 + d * 64:2 * NY * 128 + d * 64 + 64]
        col_ref[d, 128:] = jnp.concatenate([h[:32], h[32:]], axis=1).astype(bf16)


def add_kernel(keep_ref, got_ref, own_ref, out_ref):
    half = keep_ref.shape[0] // 2
    s = keep_ref[...] + got_ref[...].astype(f32)
    own_ref[...] = s[:half]
    out_ref[...] = s[half:].astype(bf16)


def add(keep, got):
    half = (keep.shape[0] // 2,) + keep.shape[1:]
    return pl.pallas_call(
        add_kernel,
        out_shape=(jax.ShapeDtypeStruct(half, f32), jax.ShapeDtypeStruct(half, bf16)),
        in_specs=[VM, VM],
        out_specs=(VM, VM),
        compiler_params=SMALL,
    )(keep, got)


def finish_rows(row_ref, out_ref):
    s = jnp.sum(row_ref[...].astype(f32), axis=0)
    out_ref[...] = jnp.concatenate([s[:, :F], s[:, F:]], axis=0)


def finish_cols(col_ref, out_ref):
    s = jnp.sum(col_ref[...].astype(f32), axis=0)
    half = jnp.concatenate([s[128:, :64], s[128:, 64:]], axis=0)
    out_ref[...] = jnp.concatenate([s[:64], s[64:128], half], axis=1)


def body(row_points, row_solves, col_points, col_probes):
    shape = jax.ShapeDtypeStruct
    rows = pl.pallas_call(
        pack_rows,
        out_shape=shape((NZ, 24, 128), bf16),
        in_specs=[VM] * 2,
        out_specs=VM,
    )(row_points, row_solves)
    cols = pl.pallas_call(
        pack_cols,
        out_shape=shape((NY, 240, 128), bf16),
        in_specs=[VM] * 2,
        out_specs=VM,
    )(col_points.T, col_probes.T)
    rows = lax.all_to_all(rows, ("zh", "zl"), 0, 0, tiled=True, axis_index_groups=[Z_ORDER])
    rows, cols = lax.optimization_barrier((rows, cols))
    cols = lax.all_to_all(cols, "y", 0, 0, tiled=True, axis_index_groups=[Y_ORDER])
    rows = lax.all_gather(rows.reshape(NZ * 24, 128), ("xa", "xb", "core"), axis=0, tiled=True)
    part = R // (2 * NX * NC)
    keep, swap, col_part = pl.pallas_call(
        main_kernel,
        out_shape=(shape((NX, part, 128), f32), shape((NX, part, 128), bf16), shape((NY, 160, 128), bf16)),
        in_specs=[VM, VM],
        out_specs=(VM, VM, VM),
        scratch_shapes=[
            pltpu.VMEM((128, C), f32),
            pltpu.VMEM((128, C), bf16),
            pltpu.VMEM((128, C), bf16),
            pltpu.VMEM((128, C), bf16),
            pltpu.VMEM((C, 128), bf16),
            pltpu.VMEM((BI, C), bf16),
            pltpu.VMEM((BI, C), bf16),
            pltpu.VMEM((128, BI), bf16),
            pltpu.VMEM((128, BI), bf16),
            pltpu.VMEM((BI, 128), f32),
            pltpu.VMEM((BI, 128), f32),
            pltpu.VMEM((2 * NX, part, 128), f32),
        ],
        compiler_params=pltpu.CompilerParams(vmem_limit_bytes=40 * 2**20),
    )(rows, cols)
    col_part = lax.all_to_all(col_part, "y", 0, 0, tiled=True, axis_index_groups=[Y_ORDER])
    keep, out = add(keep, lax.ppermute(swap, "core", [(0, 1), (1, 0)]))
    row_part = keep + lax.ppermute(out, "xb", [(0, 1), (1, 0)]).astype(f32)
    row_part = row_part.astype(bf16).reshape(2, NZ, PR // 2, 128)
    row_part = jnp.concatenate([row_part[:, TURN:], row_part[:, :TURN]], axis=1).reshape(2 * NZ, PR // 2, 128)
    row_part, col_part = lax.optimization_barrier((row_part, col_part))
    row_part = lax.all_to_all(row_part, XZ, 0, 0, tiled=True, axis_index_groups=[XZ_ORDER])
    row_grad = pl.pallas_call(
        finish_rows,
        out_shape=shape((PR, F), f32),
        in_specs=[VM],
        out_specs=VM,
        compiler_params=SMALL,
    )(row_part)
    col_grad = pl.pallas_call(
        finish_cols,
        out_shape=shape((F, PC), f32),
        in_specs=[VM],
        out_specs=VM,
        compiler_params=SMALL,
    )(col_part)
    return row_grad, col_grad.T


def solution(mesh):
    rings = Mesh(mesh.devices.reshape(SIZES), NAMES)
    row = P(("y", "zh", "xa", "xb", "zl", "core"), None)
    col = P(("xa", "xb", "zl", "core", "y", "zh"), None)
    return jax.shard_map(
        body,
        mesh=rings,
        in_specs=(row, row, col, col),
        out_specs=(row, col),
        check_vma=False,
    )
```

```python
import jax
import jax.numpy as jnp
from jax import lax
from jax.experimental import pallas as pl
from jax.experimental.pallas import tpu as pltpu
from jax.sharding import Mesh, PartitionSpec as P

f32, bf16 = jnp.float32, jnp.bfloat16

NAMES = ("y", "zh", "xa", "xb", "zl", "core")
SIZES = (8, 3, 2, 2, 4, 2)
XZ = ("xa", "zh", "zl")
Y_ORDER = [0, 2, 4, 6, 1, 3, 5, 7]
Z_ORDER = [0, 2, 4, 6, 8, 10, 1, 3, 5, 7, 9, 11]
XZ_ORDER = [12 * a + z for a in range(2) for z in Z_ORDER]
NX, NY, NZ, NC = 4, 8, 12, 2
PR, PC, F, Q = 32, 320, 64, 32
R, C = PR * NX * NZ * NC, PC * NY
NORM, ONES = F + Q, F + Q + 3
BI, BJ = R // NX, 512
PK = BI * 3 // 4

VM = pl.BlockSpec(memory_space=pltpu.VMEM)
SMALL = pltpu.CompilerParams(vmem_limit_bytes=8 * 2**20)


def thirds(v):
    a = v.astype(bf16)
    v = v - a.astype(f32)
    b = v.astype(bf16)
    return a, b, (v - b.astype(f32)).astype(bf16)


def pack_rows(rp_ref, rs_ref, row_ref):
    r, s = rp_ref[...].astype(f32), rs_ref[...].astype(f32)
    rec = jnp.concatenate(
        [
            jnp.concatenate([r[:16], r[16:]], axis=1),
            jnp.concatenate([s[:8], s[8:16], s[16:24], s[24:]], axis=1),
        ],
        axis=0,
    ).astype(bf16)
    for k in range(NZ):
        row_ref[k] = rec


def pack_cols(cp_ref, cq_ref, col_ref):
    c = jnp.concatenate([cp_ref[...].astype(f32), cq_ref[...].astype(f32) * (1.0 / Q)], axis=0)
    half = jnp.concatenate([c[:48, 256:], c[48:, 256:]], axis=1)
    piece = jnp.concatenate([c[:, :128], c[:, 128:256], half], axis=0).astype(bf16)
    for k in range(NY):
        col_ref[k] = piece


def column_records(p_ref, ct, ce, cm, cn):
    for d in range(0, NY, 2):
        for e in (d, d + 1):
            ct[:96, (2 * e) * 128:(2 * e + 1) * 128] = p_ref[e, :96]
            ct[:96, (2 * e + 1) * 128:(2 * e + 2) * 128] = p_ref[e, 96:192]
        a, b = p_ref[d, 192:240], p_ref[d + 1, 192:240]
        at = (2 * NY + d // 2) * 128
        ct[:48, at:at + 128] = jnp.concatenate([a[:, :64], b[:, :64]], axis=1)
        ct[48:96, at:at + 128] = jnp.concatenate([a[:, 64:], b[:, 64:]], axis=1)
    wide = ct[:F, :].astype(f32)
    n = -0.5 * jnp.sum(wide * wide, axis=0, keepdims=True)
    ct[96:128, :] = jnp.concatenate(
        [jnp.ones((3, C), f32)] + [p.astype(f32) for p in thirds(n)] + [jnp.zeros((26, C), f32)], axis=0
    ).astype(bf16)
    ce[...] = ct[...]
    ce[F:F + Q, :] = jnp.zeros((Q, C), bf16)
    cm[...] = jnp.zeros_like(cm)
    cm[F:F + Q, :] = ct[F:F + Q, :]
    cn[...] = ce[...].T


def row_records(packed):
    n = packed.shape[0] // 24
    rec = packed.astype(f32).reshape(n, 24, 128)
    points, solves = rec[:, :16], rec[:, 16:]

    def roll(x, k):
        return pltpu.roll(x.reshape(-1, 128), k, 1).reshape(x.shape)

    r = jnp.stack([points, roll(points, 64)], axis=1).reshape(n * PR, 128)
    s = jnp.stack([roll(solves, 64), roll(solves, 32), solves, roll(solves, 96)], axis=1).reshape(n * PR, 128)
    lane = lax.broadcasted_iota(jnp.int32, (n * PR, 128), 1)
    r = jnp.where(lane < F, r, 0.0)
    a, b, c = [t.astype(f32) for t in thirds(-0.5 * jnp.sum(r * r, axis=1, keepdims=True))]
    ext = jnp.where(lane < ONES + 3, 1.0, 0.0)
    ext = jnp.where(lane == NORM, a, jnp.where(lane == NORM + 1, b, jnp.where(lane == NORM + 2, c, ext)))
    return r, jnp.where(lane < F, r, jnp.where(lane < NORM, s, ext)).astype(bf16)


def main_kernel(r_ref, p_ref, keep_ref, swap_ref, col_ref, acc_c, ct, ce, cm, cn, w0, w1, rt0, rt1, rf0, rf1, part):
    column_records(p_ref, ct, ce, cm, cn)
    acc_c[...] = jnp.zeros_like(acc_c)
    bufs = ((w0, rt0, rf0), (w1, rt1, rf1))
    n = R // BI
    xb, core = lax.axis_index("xb"), lax.axis_index("core")

    def front(i, buf):
        r, rb = row_records(r_ref[pl.ds(pl.multiple_of(i * PK, PK), PK), :])
        buf[1][...] = rb.T
        buf[2][...] = r
        return rb

    def weights(rb, j, buf):
        e = jnp.dot(rb, ce[:, j:j + BJ], preferred_element_type=f32)
        m = jnp.dot(rb, cm[:, j:j + BJ], preferred_element_type=f32)
        buf[0][:, j:j + BJ] = (jnp.exp(e) * m).astype(bf16)

    def columns(j, buf):
        acc_c[:, j:j + BJ] += jnp.dot(buf[1][...], buf[0][:, j:j + BJ], preferred_element_type=f32)

    def rows(i, buf):
        a = jnp.dot(buf[0][...], cn[...], preferred_element_type=f32)
        t = a[:, :F] - a[:, NORM:NORM + 1] * buf[2][:, :F]
        t = t.reshape(BI // PR, 2, PR // 2, F)
        t = jnp.concatenate([t[:, 0], t[:, 1]], axis=-1).reshape(BI // 2, 128)
        at = 2 * jnp.int32(i % 2 != xb) + i // 2
        for h in range(2):
            part[at + 4 * jnp.int32(h != core)] = t[h * (BI // 4):(h + 1) * (BI // 4)]

    def both(i, new, old):
        rb = front(i, new)
        for j in range(0, C, BJ):
            weights(rb, j, new)
            columns(j, old)
        rows(i - 1, old)

    rb = front(0, bufs[0])
    for j in range(0, C, BJ):
        weights(rb, j, bufs[0])

    def step(k, carry):
        both(2 * k + 1, bufs[1], bufs[0])
        both(2 * k + 2, bufs[0], bufs[1])
        return carry

    lax.fori_loop(0, (n - 2) // 2, step, 0)
    both(n - 1, bufs[1], bufs[0])
    for j in range(0, C, BJ):
        columns(j, bufs[1])
    rows(n - 1, bufs[1])

    keep_ref[...] = part[:4]
    swap_ref[...] = part[4:].astype(bf16)
    u = acc_c[:F, :] - acc_c[ONES:ONES + 1, :] * ct[:F, :].astype(f32)

    for d in range(NY):
        col_ref[d, :64] = u[:, (2 * d) * 128:(2 * d + 1) * 128].astype(bf16)
        col_ref[d, 64:128] = u[:, (2 * d + 1) * 128:(2 * d + 2) * 128].astype(bf16)
        h = u[:, 2 * NY * 128 + d * 64:2 * NY * 128 + d * 64 + 64]
        col_ref[d, 128:] = jnp.concatenate([h[:32], h[32:]], axis=1).astype(bf16)


def add_kernel(keep_ref, got_ref, own_ref, out_ref):
    half = keep_ref.shape[0] // 2
    s = keep_ref[...] + got_ref[...].astype(f32)
    own_ref[...] = s[:half]
    out_ref[...] = s[half:].astype(bf16)


def add(keep, got):
    half = (keep.shape[0] // 2,) + keep.shape[1:]
    return pl.pallas_call(
        add_kernel,
        out_shape=(jax.ShapeDtypeStruct(half, f32), jax.ShapeDtypeStruct(half, bf16)),
        in_specs=[VM, VM],
        out_specs=(VM, VM),
        compiler_params=SMALL,
    )(keep, got)


def finish_rows(row_ref, out_ref):
    s = jnp.sum(row_ref[...].astype(f32), axis=0)
    out_ref[...] = jnp.concatenate([s[:, :F], s[:, F:]], axis=0)


def finish_cols(col_ref, out_ref):
    s = jnp.sum(col_ref[...].astype(f32), axis=0)
    half = jnp.concatenate([s[128:, :64], s[128:, 64:]], axis=0)
    out_ref[...] = jnp.concatenate([s[:64], s[64:128], half], axis=1)


def body(row_points, row_solves, col_points, col_probes):
    shape = jax.ShapeDtypeStruct
    rows = pl.pallas_call(
        pack_rows,
        out_shape=shape((NZ, 24, 128), bf16),
        in_specs=[VM] * 2,
        out_specs=VM,
    )(row_points, row_solves)
    cols = pl.pallas_call(
        pack_cols,
        out_shape=shape((NY, 240, 128), bf16),
        in_specs=[VM] * 2,
        out_specs=VM,
    )(col_points.T, col_probes.T)
    rows = lax.all_to_all(rows, ("zh", "zl"), 0, 0, tiled=True, axis_index_groups=[Z_ORDER])
    rows, cols = lax.optimization_barrier((rows, cols))
    cols = lax.all_to_all(cols, "y", 0, 0, tiled=True, axis_index_groups=[Y_ORDER])
    rows = lax.all_gather(rows.reshape(NZ * 24, 128), ("xa", "xb", "core"), axis=0, tiled=True)
    part = R // (2 * NX * NC)
    keep, swap, col_part = pl.pallas_call(
        main_kernel,
        out_shape=(shape((NX, part, 128), f32), shape((NX, part, 128), bf16), shape((NY, 160, 128), bf16)),
        in_specs=[VM, VM],
        out_specs=(VM, VM, VM),
        scratch_shapes=[
            pltpu.VMEM((128, C), f32),
            pltpu.VMEM((128, C), bf16),
            pltpu.VMEM((128, C), bf16),
            pltpu.VMEM((128, C), bf16),
            pltpu.VMEM((C, 128), bf16),
            pltpu.VMEM((BI, C), bf16),
            pltpu.VMEM((BI, C), bf16),
            pltpu.VMEM((128, BI), bf16),
            pltpu.VMEM((128, BI), bf16),
            pltpu.VMEM((BI, 128), f32),
            pltpu.VMEM((BI, 128), f32),
            pltpu.VMEM((2 * NX, part, 128), f32),
        ],
        compiler_params=pltpu.CompilerParams(vmem_limit_bytes=40 * 2**20),
    )(rows, cols)
    col_part = lax.all_to_all(col_part, "y", 0, 0, tiled=True, axis_index_groups=[Y_ORDER])
    keep, out = add(keep, lax.ppermute(swap, "core", [(0, 1), (1, 0)]))
    row_part = keep + lax.ppermute(out, "xb", [(0, 1), (1, 0)]).astype(f32)
    row_part = row_part.astype(bf16).reshape(2 * NZ, PR // 2, 128)
    row_part, col_part = lax.optimization_barrier((row_part, col_part))
    row_part = lax.all_to_all(row_part, XZ, 0, 0, tiled=True, axis_index_groups=[XZ_ORDER])
    row_grad = pl.pallas_call(
        finish_rows,
        out_shape=shape((PR, F), f32),
        in_specs=[VM],
        out_specs=VM,
        compiler_params=SMALL,
    )(row_part)
    col_grad = pl.pallas_call(
        finish_cols,
        out_shape=shape((F, PC), f32),
        in_specs=[VM],
        out_specs=VM,
        compiler_params=SMALL,
    )(col_part)
    return row_grad, col_grad.T


def solution(mesh):
    rings = Mesh(mesh.devices.reshape(SIZES), NAMES)
    row = P(("y", "zh", "xa", "xb", "zl", "core"), None)
    col = P(("xa", "xb", "zl", "core", "y", "zh"), None)
    return jax.shard_map(
        body,
        mesh=rings,
        in_specs=(row, row, col, col),
        out_specs=(row, col),
        check_vma=False,
    )
```

```python
import jax
import jax.numpy as jnp
from jax import lax
from jax.experimental import pallas as pl
from jax.experimental.pallas import tpu as pltpu
from jax.sharding import Mesh, PartitionSpec as P

f32, bf16 = jnp.float32, jnp.bfloat16

NAMES = ("y", "zh", "xa", "xb", "zl", "core")
SIZES = (8, 3, 2, 2, 4, 2)
XZ = ("xa", "zh", "zl")
Y_ORDER = [0, 2, 4, 6, 1, 3, 5, 7]
Z_ORDER = [0, 2, 4, 6, 8, 10, 1, 3, 5, 7, 9, 11]
NX, NY, NZ, NC = 4, 8, 12, 2
PR, PC, F, Q = 32, 320, 64, 32
R, C = PR * NX * NZ * NC, PC * NY
NORM, ONES = F + Q, F + Q + 3
BI, BJ = R // NX, 512
PK = BI * 3 // 4

VM = pl.BlockSpec(memory_space=pltpu.VMEM)
SMALL = pltpu.CompilerParams(vmem_limit_bytes=8 * 2**20)


def thirds(v):
    a = v.astype(bf16)
    v = v - a.astype(f32)
    b = v.astype(bf16)
    return a, b, (v - b.astype(f32)).astype(bf16)


def pack_rows(rp_ref, rs_ref, row_ref):
    r, s = rp_ref[...].astype(f32), rs_ref[...].astype(f32)
    rec = jnp.concatenate(
        [
            jnp.concatenate([r[:16], r[16:]], axis=1),
            jnp.concatenate([s[:8], s[8:16], s[16:24], s[24:]], axis=1),
        ],
        axis=0,
    ).astype(bf16)
    for k in range(NZ):
        row_ref[k] = rec


def pack_cols(cp_ref, cq_ref, col_ref):
    c = jnp.concatenate([cp_ref[...].astype(f32), cq_ref[...].astype(f32) * (1.0 / Q)], axis=0)
    half = jnp.concatenate([c[:48, 256:], c[48:, 256:]], axis=1)
    piece = jnp.concatenate([c[:, :128], c[:, 128:256], half], axis=0).astype(bf16)
    for k in range(NY):
        col_ref[k] = piece


def column_records(p_ref, ct, ce, cm, cn):
    for d in range(0, NY, 2):
        for e in (d, d + 1):
            ct[:96, (2 * e) * 128:(2 * e + 1) * 128] = p_ref[e, :96]
            ct[:96, (2 * e + 1) * 128:(2 * e + 2) * 128] = p_ref[e, 96:192]
        a, b = p_ref[d, 192:240], p_ref[d + 1, 192:240]
        at = (2 * NY + d // 2) * 128
        ct[:48, at:at + 128] = jnp.concatenate([a[:, :64], b[:, :64]], axis=1)
        ct[48:96, at:at + 128] = jnp.concatenate([a[:, 64:], b[:, 64:]], axis=1)
    wide = ct[:F, :].astype(f32)
    n = -0.5 * jnp.sum(wide * wide, axis=0, keepdims=True)
    ct[96:128, :] = jnp.concatenate(
        [jnp.ones((3, C), f32)] + [p.astype(f32) for p in thirds(n)] + [jnp.zeros((26, C), f32)], axis=0
    ).astype(bf16)
    ce[...] = ct[...]
    ce[F:F + Q, :] = jnp.zeros((Q, C), bf16)
    cm[...] = jnp.zeros_like(cm)
    cm[F:F + Q, :] = ct[F:F + Q, :]
    cn[...] = ce[...].T


def row_records(packed):
    n = packed.shape[0] // 24
    rec = packed.astype(f32).reshape(n, 24, 128)
    points, solves = rec[:, :16], rec[:, 16:]

    def roll(x, k):
        return pltpu.roll(x.reshape(-1, 128), k, 1).reshape(x.shape)

    r = jnp.stack([points, roll(points, 64)], axis=1).reshape(n * PR, 128)
    s = jnp.stack([roll(solves, 64), roll(solves, 32), solves, roll(solves, 96)], axis=1).reshape(n * PR, 128)
    lane = lax.broadcasted_iota(jnp.int32, (n * PR, 128), 1)
    r = jnp.where(lane < F, r, 0.0)
    a, b, c = [t.astype(f32) for t in thirds(-0.5 * jnp.sum(r * r, axis=1, keepdims=True))]
    ext = jnp.where(lane < ONES + 3, 1.0, 0.0)
    ext = jnp.where(lane == NORM, a, jnp.where(lane == NORM + 1, b, jnp.where(lane == NORM + 2, c, ext)))
    return r, jnp.where(lane < F, r, jnp.where(lane < NORM, s, ext)).astype(bf16)


def main_kernel(r_ref, p_ref, keep_ref, swap_ref, col_ref, acc_c, ct, ce, cm, cn, w0, w1, rt0, rt1, rf0, rf1, part):
    column_records(p_ref, ct, ce, cm, cn)
    acc_c[...] = jnp.zeros_like(acc_c)
    bufs = ((w0, rt0, rf0), (w1, rt1, rf1))
    n = R // BI
    xb, core = lax.axis_index("xb"), lax.axis_index("core")

    def front(i, buf):
        r, rb = row_records(r_ref[pl.ds(pl.multiple_of(i * PK, PK), PK), :])
        buf[1][...] = rb.T
        buf[2][...] = r
        return rb

    def weights(rb, j, buf):
        e = jnp.dot(rb, ce[:, j:j + BJ], preferred_element_type=f32)
        m = jnp.dot(rb, cm[:, j:j + BJ], preferred_element_type=f32)
        buf[0][:, j:j + BJ] = (jnp.exp(e) * m).astype(bf16)

    def columns(j, buf):
        acc_c[:, j:j + BJ] += jnp.dot(buf[1][...], buf[0][:, j:j + BJ], preferred_element_type=f32)

    def rows(i, buf):
        a = jnp.dot(buf[0][...], cn[...], preferred_element_type=f32)
        t = a[:, :F] - a[:, NORM:NORM + 1] * buf[2][:, :F]
        t = t.reshape(BI // PR, 2, PR // 2, F)
        t = jnp.concatenate([t[:, 0], t[:, 1]], axis=-1).reshape(BI // 2, 128)
        at = 2 * jnp.int32(i % 2 != xb) + i // 2
        for h in range(2):
            v = t[h * (BI // 4):(h + 1) * (BI // 4)].reshape(2, NZ // 2, PR // 2, 128)
            part[at + 4 * jnp.int32(h != core)] = jnp.stack([v[0], v[1]], axis=1).reshape(BI // 4, 128)

    def both(i, new, old):
        rb = front(i, new)
        for j in range(0, C, BJ):
            weights(rb, j, new)
            columns(j, old)
        rows(i - 1, old)

    rb = front(0, bufs[0])
    for j in range(0, C, BJ):
        weights(rb, j, bufs[0])

    def step(k, carry):
        both(2 * k + 1, bufs[1], bufs[0])
        both(2 * k + 2, bufs[0], bufs[1])
        return carry

    lax.fori_loop(0, (n - 2) // 2, step, 0)
    both(n - 1, bufs[1], bufs[0])
    for j in range(0, C, BJ):
        columns(j, bufs[1])
    rows(n - 1, bufs[1])

    keep_ref[...] = part[:4]
    swap_ref[...] = part[4:].astype(bf16)
    u = acc_c[:F, :] - acc_c[ONES:ONES + 1, :] * ct[:F, :].astype(f32)

    for d in range(NY):
        col_ref[d, :64] = u[:, (2 * d) * 128:(2 * d + 1) * 128].astype(bf16)
        col_ref[d, 64:128] = u[:, (2 * d + 1) * 128:(2 * d + 2) * 128].astype(bf16)
        h = u[:, 2 * NY * 128 + d * 64:2 * NY * 128 + d * 64 + 64]
        col_ref[d, 128:] = jnp.concatenate([h[:32], h[32:]], axis=1).astype(bf16)


def add_kernel(keep_ref, got_ref, own_ref, out_ref):
    half = keep_ref.shape[0] // 2
    s = keep_ref[...] + got_ref[...].astype(f32)
    own_ref[...] = s[:half]
    out_ref[...] = s[half:].astype(bf16)


def add(keep, got):
    half = (keep.shape[0] // 2,) + keep.shape[1:]
    return pl.pallas_call(
        add_kernel,
        out_shape=(jax.ShapeDtypeStruct(half, f32), jax.ShapeDtypeStruct(half, bf16)),
        in_specs=[VM, VM],
        out_specs=(VM, VM),
        compiler_params=SMALL,
    )(keep, got)


def finish_rows(row_ref, out_ref):
    s = jnp.sum(row_ref[...].astype(f32), axis=0)
    out_ref[...] = jnp.concatenate([s[:, :F], s[:, F:]], axis=0)


def finish_cols(col_ref, out_ref):
    s = jnp.sum(col_ref[...].astype(f32), axis=0)
    half = jnp.concatenate([s[128:, :64], s[128:, 64:]], axis=0)
    out_ref[...] = jnp.concatenate([s[:64], s[64:128], half], axis=1)


def body(row_points, row_solves, col_points, col_probes):
    shape = jax.ShapeDtypeStruct
    rows = pl.pallas_call(
        pack_rows,
        out_shape=shape((NZ, 24, 128), bf16),
        in_specs=[VM] * 2,
        out_specs=VM,
    )(row_points, row_solves)
    cols = pl.pallas_call(
        pack_cols,
        out_shape=shape((NY, 240, 128), bf16),
        in_specs=[VM] * 2,
        out_specs=VM,
    )(col_points.T, col_probes.T)
    rows = lax.all_to_all(rows, ("zh", "zl"), 0, 0, tiled=True, axis_index_groups=[Z_ORDER])
    rows, cols = lax.optimization_barrier((rows, cols))
    cols = lax.all_to_all(cols, "y", 0, 0, tiled=True, axis_index_groups=[Y_ORDER])
    rows = lax.all_gather(rows.reshape(NZ * 24, 128), ("xa", "xb", "core"), axis=0, tiled=True)
    part = R // (2 * NX * NC)
    keep, swap, col_part = pl.pallas_call(
        main_kernel,
        out_shape=(shape((NX, part, 128), f32), shape((NX, part, 128), bf16), shape((NY, 160, 128), bf16)),
        in_specs=[VM, VM],
        out_specs=(VM, VM, VM),
        scratch_shapes=[
            pltpu.VMEM((128, C), f32),
            pltpu.VMEM((128, C), bf16),
            pltpu.VMEM((128, C), bf16),
            pltpu.VMEM((128, C), bf16),
            pltpu.VMEM((C, 128), bf16),
            pltpu.VMEM((BI, C), bf16),
            pltpu.VMEM((BI, C), bf16),
            pltpu.VMEM((128, BI), bf16),
            pltpu.VMEM((128, BI), bf16),
            pltpu.VMEM((BI, 128), f32),
            pltpu.VMEM((BI, 128), f32),
            pltpu.VMEM((2 * NX, part, 128), f32),
        ],
        compiler_params=pltpu.CompilerParams(vmem_limit_bytes=40 * 2**20),
    )(rows, cols)
    col_part = lax.all_to_all(col_part, "y", 0, 0, tiled=True, axis_index_groups=[Y_ORDER])
    keep, out = add(keep, lax.ppermute(swap, "core", [(0, 1), (1, 0)]))
    row_part = keep + lax.ppermute(out, "xb", [(0, 1), (1, 0)]).astype(f32)
    row_part = row_part.astype(bf16).reshape(2 * NZ, PR // 2, 128)
    row_part, col_part = lax.optimization_barrier((row_part, col_part))
    row_part = lax.all_to_all(row_part, XZ, 0, 0, tiled=True)
    row_grad = pl.pallas_call(
        finish_rows,
        out_shape=shape((PR, F), f32),
        in_specs=[VM],
        out_specs=VM,
        compiler_params=SMALL,
    )(row_part)
    col_grad = pl.pallas_call(
        finish_cols,
        out_shape=shape((F, PC), f32),
        in_specs=[VM],
        out_specs=VM,
        compiler_params=SMALL,
    )(col_part)
    return row_grad, col_grad.T


def solution(mesh):
    rings = Mesh(mesh.devices.reshape(SIZES), NAMES)
    row = P(("y", "zh", "xa", "xb", "zl", "core"), None)
    col = P(("xa", "xb", "zl", "core", "y", "zh"), None)
    return jax.shard_map(
        body,
        mesh=rings,
        in_specs=(row, row, col, col),
        out_specs=(row, col),
        check_vma=False,
    )
```

```python
import jax
import jax.numpy as jnp
from jax import lax
from jax.experimental import pallas as pl
from jax.experimental.pallas import tpu as pltpu
from jax.sharding import Mesh, PartitionSpec as P

f32, bf16 = jnp.float32, jnp.bfloat16

NAMES = ("y", "zh", "xa", "xb", "zl", "core")
SIZES = (8, 3, 2, 2, 4, 2)
XZ = ("xa", "zh", "zl")
Y_ORDER = [0, 4, 1, 5, 2, 6, 3, 7]
Z_ORDER = [0, 2, 4, 6, 8, 10, 1, 3, 5, 7, 9, 11]
NX, NY, NZ, NC = 4, 8, 12, 2
PR, PC, F, Q = 32, 320, 64, 32
R, C = PR * NX * NZ * NC, PC * NY
NORM, ONES = F + Q, F + Q + 3
BI, BJ = R // NX, 512
PK = BI * 3 // 4

VM = pl.BlockSpec(memory_space=pltpu.VMEM)
SMALL = pltpu.CompilerParams(vmem_limit_bytes=8 * 2**20)


def thirds(v):
    a = v.astype(bf16)
    v = v - a.astype(f32)
    b = v.astype(bf16)
    return a, b, (v - b.astype(f32)).astype(bf16)


def pack_rows(rp_ref, rs_ref, row_ref):
    r, s = rp_ref[...].astype(f32), rs_ref[...].astype(f32)
    rec = jnp.concatenate(
        [
            jnp.concatenate([r[:16], r[16:]], axis=1),
            jnp.concatenate([s[:8], s[8:16], s[16:24], s[24:]], axis=1),
        ],
        axis=0,
    ).astype(bf16)
    for k in range(NZ):
        row_ref[k] = rec


def pack_cols(cp_ref, cq_ref, col_ref):
    c = jnp.concatenate([cp_ref[...].astype(f32), cq_ref[...].astype(f32) * (1.0 / Q)], axis=0)
    half = jnp.concatenate([c[:48, 256:], c[48:, 256:]], axis=1)
    piece = jnp.concatenate([c[:, :128], c[:, 128:256], half], axis=0).astype(bf16)
    for k in range(NY):
        col_ref[k] = piece


def column_records(p_ref, ct, ce, cm, cn):
    for d in range(0, NY, 2):
        for e in (d, d + 1):
            ct[:96, (2 * e) * 128:(2 * e + 1) * 128] = p_ref[e, :96]
            ct[:96, (2 * e + 1) * 128:(2 * e + 2) * 128] = p_ref[e, 96:192]
        a, b = p_ref[d, 192:240], p_ref[d + 1, 192:240]
        at = (2 * NY + d // 2) * 128
        ct[:48, at:at + 128] = jnp.concatenate([a[:, :64], b[:, :64]], axis=1)
        ct[48:96, at:at + 128] = jnp.concatenate([a[:, 64:], b[:, 64:]], axis=1)
    wide = ct[:F, :].astype(f32)
    n = -0.5 * jnp.sum(wide * wide, axis=0, keepdims=True)
    ct[96:128, :] = jnp.concatenate(
        [jnp.ones((3, C), f32)] + [p.astype(f32) for p in thirds(n)] + [jnp.zeros((26, C), f32)], axis=0
    ).astype(bf16)
    ce[...] = ct[...]
    ce[F:F + Q, :] = jnp.zeros((Q, C), bf16)
    cm[...] = jnp.zeros_like(cm)
    cm[F:F + Q, :] = ct[F:F + Q, :]
    cn[...] = ce[...].T


def row_records(packed):
    n = packed.shape[0] // 24
    rec = packed.astype(f32).reshape(n, 24, 128)
    points, solves = rec[:, :16], rec[:, 16:]

    def roll(x, k):
        return pltpu.roll(x.reshape(-1, 128), k, 1).reshape(x.shape)

    r = jnp.stack([points, roll(points, 64)], axis=1).reshape(n * PR, 128)
    s = jnp.stack([roll(solves, 64), roll(solves, 32), solves, roll(solves, 96)], axis=1).reshape(n * PR, 128)
    lane = lax.broadcasted_iota(jnp.int32, (n * PR, 128), 1)
    r = jnp.where(lane < F, r, 0.0)
    a, b, c = [t.astype(f32) for t in thirds(-0.5 * jnp.sum(r * r, axis=1, keepdims=True))]
    ext = jnp.where(lane < ONES + 3, 1.0, 0.0)
    ext = jnp.where(lane == NORM, a, jnp.where(lane == NORM + 1, b, jnp.where(lane == NORM + 2, c, ext)))
    return r, jnp.where(lane < F, r, jnp.where(lane < NORM, s, ext)).astype(bf16)


def main_kernel(r_ref, p_ref, keep_ref, swap_ref, col_ref, acc_c, ct, ce, cm, cn, w0, w1, rt0, rt1, rf0, rf1, part):
    column_records(p_ref, ct, ce, cm, cn)
    acc_c[...] = jnp.zeros_like(acc_c)
    bufs = ((w0, rt0, rf0), (w1, rt1, rf1))
    n = R // BI
    xb, core = lax.axis_index("xb"), lax.axis_index("core")

    def front(i, buf):
        r, rb = row_records(r_ref[pl.ds(pl.multiple_of(i * PK, PK), PK), :])
        buf[1][...] = rb.T
        buf[2][...] = r
        return rb

    def weights(rb, j, buf):
        e = jnp.dot(rb, ce[:, j:j + BJ], preferred_element_type=f32)
        m = jnp.dot(rb, cm[:, j:j + BJ], preferred_element_type=f32)
        buf[0][:, j:j + BJ] = (jnp.exp(e) * m).astype(bf16)

    def columns(j, buf):
        acc_c[:, j:j + BJ] += jnp.dot(buf[1][...], buf[0][:, j:j + BJ], preferred_element_type=f32)

    def rows(i, buf):
        a = jnp.dot(buf[0][...], cn[...], preferred_element_type=f32)
        t = a[:, :F] - a[:, NORM:NORM + 1] * buf[2][:, :F]
        t = t.reshape(BI // PR, 2, PR // 2, F)
        t = jnp.concatenate([t[:, 0], t[:, 1]], axis=-1).reshape(BI // 2, 128)
        at = 2 * jnp.int32(i % 2 != xb) + i // 2
        for h in range(2):
            v = t[h * (BI // 4):(h + 1) * (BI // 4)].reshape(2, NZ // 2, PR // 2, 128)
            part[at + 4 * jnp.int32(h != core)] = jnp.stack([v[0], v[1]], axis=1).reshape(BI // 4, 128)

    def both(i, new, old):
        rb = front(i, new)
        for j in range(0, C, BJ):
            weights(rb, j, new)
            columns(j, old)
        rows(i - 1, old)

    rb = front(0, bufs[0])
    for j in range(0, C, BJ):
        weights(rb, j, bufs[0])

    def step(k, carry):
        both(2 * k + 1, bufs[1], bufs[0])
        both(2 * k + 2, bufs[0], bufs[1])
        return carry

    lax.fori_loop(0, (n - 2) // 2, step, 0)
    both(n - 1, bufs[1], bufs[0])
    for j in range(0, C, BJ):
        columns(j, bufs[1])
    rows(n - 1, bufs[1])

    keep_ref[...] = part[:4]
    swap_ref[...] = part[4:].astype(bf16)
    u = acc_c[:F, :] - acc_c[ONES:ONES + 1, :] * ct[:F, :].astype(f32)

    for d in range(NY):
        col_ref[d, :64] = u[:, (2 * d) * 128:(2 * d + 1) * 128].astype(bf16)
        col_ref[d, 64:128] = u[:, (2 * d + 1) * 128:(2 * d + 2) * 128].astype(bf16)
        h = u[:, 2 * NY * 128 + d * 64:2 * NY * 128 + d * 64 + 64]
        col_ref[d, 128:] = jnp.concatenate([h[:32], h[32:]], axis=1).astype(bf16)


def add_kernel(keep_ref, got_ref, own_ref, out_ref):
    half = keep_ref.shape[0] // 2
    s = keep_ref[...] + got_ref[...].astype(f32)
    own_ref[...] = s[:half]
    out_ref[...] = s[half:].astype(bf16)


def add(keep, got):
    half = (keep.shape[0] // 2,) + keep.shape[1:]
    return pl.pallas_call(
        add_kernel,
        out_shape=(jax.ShapeDtypeStruct(half, f32), jax.ShapeDtypeStruct(half, bf16)),
        in_specs=[VM, VM],
        out_specs=(VM, VM),
        compiler_params=SMALL,
    )(keep, got)


def finish_rows(row_ref, out_ref):
    s = jnp.sum(row_ref[...].astype(f32), axis=0)
    out_ref[...] = jnp.concatenate([s[:, :F], s[:, F:]], axis=0)


def finish_cols(col_ref, out_ref):
    s = jnp.sum(col_ref[...].astype(f32), axis=0)
    half = jnp.concatenate([s[128:, :64], s[128:, 64:]], axis=0)
    out_ref[...] = jnp.concatenate([s[:64], s[64:128], half], axis=1)


def body(row_points, row_solves, col_points, col_probes):
    shape = jax.ShapeDtypeStruct
    rows = pl.pallas_call(
        pack_rows,
        out_shape=shape((NZ, 24, 128), bf16),
        in_specs=[VM] * 2,
        out_specs=VM,
    )(row_points, row_solves)
    cols = pl.pallas_call(
        pack_cols,
        out_shape=shape((NY, 240, 128), bf16),
        in_specs=[VM] * 2,
        out_specs=VM,
    )(col_points.T, col_probes.T)
    rows = lax.all_to_all(rows, ("zh", "zl"), 0, 0, tiled=True, axis_index_groups=[Z_ORDER])
    rows, cols = lax.optimization_barrier((rows, cols))
    cols = lax.all_to_all(cols, "y", 0, 0, tiled=True, axis_index_groups=[Y_ORDER])
    rows = lax.all_gather(rows.reshape(NZ * 24, 128), ("xa", "xb", "core"), axis=0, tiled=True)
    part = R // (2 * NX * NC)
    keep, swap, col_part = pl.pallas_call(
        main_kernel,
        out_shape=(shape((NX, part, 128), f32), shape((NX, part, 128), bf16), shape((NY, 160, 128), bf16)),
        in_specs=[VM, VM],
        out_specs=(VM, VM, VM),
        scratch_shapes=[
            pltpu.VMEM((128, C), f32),
            pltpu.VMEM((128, C), bf16),
            pltpu.VMEM((128, C), bf16),
            pltpu.VMEM((128, C), bf16),
            pltpu.VMEM((C, 128), bf16),
            pltpu.VMEM((BI, C), bf16),
            pltpu.VMEM((BI, C), bf16),
            pltpu.VMEM((128, BI), bf16),
            pltpu.VMEM((128, BI), bf16),
            pltpu.VMEM((BI, 128), f32),
            pltpu.VMEM((BI, 128), f32),
            pltpu.VMEM((2 * NX, part, 128), f32),
        ],
        compiler_params=pltpu.CompilerParams(vmem_limit_bytes=40 * 2**20),
    )(rows, cols)
    col_part = lax.all_to_all(col_part, "y", 0, 0, tiled=True, axis_index_groups=[Y_ORDER])
    keep, out = add(keep, lax.ppermute(swap, "core", [(0, 1), (1, 0)]))
    row_part = keep + lax.ppermute(out, "xb", [(0, 1), (1, 0)]).astype(f32)
    row_part = row_part.astype(bf16).reshape(2 * NZ, PR // 2, 128)
    row_part, col_part = lax.optimization_barrier((row_part, col_part))
    row_part = lax.all_to_all(row_part, XZ, 0, 0, tiled=True)
    row_grad = pl.pallas_call(
        finish_rows,
        out_shape=shape((PR, F), f32),
        in_specs=[VM],
        out_specs=VM,
        compiler_params=SMALL,
    )(row_part)
    col_grad = pl.pallas_call(
        finish_cols,
        out_shape=shape((F, PC), f32),
        in_specs=[VM],
        out_specs=VM,
        compiler_params=SMALL,
    )(col_part)
    return row_grad, col_grad.T


def solution(mesh):
    rings = Mesh(mesh.devices.reshape(SIZES), NAMES)
    row = P(("y", "zh", "xa", "xb", "zl", "core"), None)
    col = P(("xa", "xb", "zl", "core", "y", "zh"), None)
    return jax.shard_map(
        body,
        mesh=rings,
        in_specs=(row, row, col, col),
        out_specs=(row, col),
        check_vma=False,
    )
```
